256 devices in a mesh: cell: 32 (over x, z), samp: 8 (over y, core).
Axes of the slice: x: 4, y: 4, z: 8, core: 2. Of those that a mesh axis runs over, the one named last changes fastest.
Arguments:
- bases: float32 [16, 65536, 192], P('samp', 'cell'), may hold values from -12 to 12
- reference_basis: float32 [65536, 192], P(('cell', 'samp')), may hold values from -5 to 5
- mass: float32 [65536], P('cell'), may hold values from 0.25 to 2.5
- interp_weights: float32 [16], P('samp'), may hold values from 0.2 to 1
Outputs:
- tangent: float32 [65536, 192], P(('cell', 'samp'))
The draws below stay inside these ranges and needn't reach their ends.
All inputs are finite; a program needn't handle non-finite values.
Results may differ from the reference program's by a relative error of at most 0.0003.
Values sent between devices are 32-bit elements; how exact they have to be, the bound alone decides.
A program may use at most 64 MiB of HBM per device.

```python
import math
import jax
import jax.numpy as jnp
from jax import lax

R = 192
K = 16
NTERMS = 6
NROWS = 65536


def shared_panel(key):
    sub_key = jax.random.fold_in(key, 11)
    values = jnp.clip(jax.random.normal(sub_key, (NROWS, R), jnp.float32), -5.0, 5.0)
    return values


def draw_reference_basis(key, part):
    return shared_panel(key)


def draw_bases(key, part):
    panel_rows = shared_panel(key)
    identity = jnp.eye(R, dtype=jnp.float32)
    stretch = jnp.exp(jax.random.uniform(jax.random.fold_in(key, 21), (K, R), jnp.float32, math.log(0.6), math.log(1.6)))
    mixing = stretch[:, :, None] * identity + 0.15 * jnp.clip(jax.random.normal(jax.random.fold_in(key, 22), (K, R, R), jnp.float32), -4.0, 4.0) / math.sqrt(R)
    spread = jnp.exp(jax.random.uniform(jax.random.fold_in(key, 23), (K, R), jnp.float32, math.log(0.15), math.log(0.7)))
    turning = spread[:, :, None] * identity + 0.1 * jnp.clip(jax.random.normal(jax.random.fold_in(key, 24), (K, R, R), jnp.float32), -4.0, 4.0) / math.sqrt(R)
    noise = jnp.clip(jax.random.normal(jax.random.fold_in(key, 25), (K, NROWS, R), jnp.float32), -4.0, 4.0)
    result = jnp.einsum('nr,krq->knq', panel_rows, mixing, precision=lax.Precision.HIGHEST)
    result = result + jnp.einsum('knr,krq->knq', noise, turning, precision=lax.Precision.HIGHEST)
    return jnp.clip(result, -12.0, 12.0)


def shard_levels(rng, extent, cuts, low, largest):
    def one(dim, blocks):
        steps = jax.random.uniform(jax.random.fold_in(jax.random.fold_in(rng, 6), dim), (blocks,), jnp.float32, low / len(cuts), largest / len(cuts))
        return jnp.repeat(jnp.exp(steps), extent[dim] // blocks).reshape((-1,) + (1,) * (len(extent) - dim - 1))

    factor_of = one(*cuts[0])
    for cut in cuts[1:]:
        factor_of = factor_of * one(*cut)
    return factor_of


def setup_inputs(seed: int = 0) -> dict:
    arg_keys = jax.random.split(jax.random.key(seed), 5)
    bases = draw_bases(jax.random.fold_in(arg_keys[4], 71), 0)
    reference_basis = draw_reference_basis(jax.random.fold_in(arg_keys[4], 71), 0)
    mass = jnp.clip(jnp.exp(math.log(2.5) - 2.3025851 * jax.random.uniform(arg_keys[2], (NROWS,), jnp.float32) ** shard_levels(arg_keys[2], (NROWS,), ((0, 32),), -0.2, 0.2)), 0.25, 2.5)
    interp_weights = jnp.clip(0.2 + 0.8 * jax.random.uniform(arg_keys[3], (K,), jnp.float32) ** shard_levels(arg_keys[3], (K,), ((0, 8),), -0.2, 0.2), 0.2, 1.0)
    return {"bases": bases, "reference_basis": reference_basis, "mass": mass, "interp_weights": interp_weights}


HIGHEST_PRECISION = lax.Precision.HIGHEST

def invert(matrix):
    normal_matrix = jnp.matmul(matrix.T, matrix, precision=HIGHEST_PRECISION)
    factor = jnp.linalg.cholesky(normal_matrix)
    return jax.scipy.linalg.cho_solve((factor, True), matrix.T)

def series(curvature_gram):
    identity = jnp.eye(curvature_gram.shape[-1], dtype=curvature_gram.dtype)
    leading = (-1.0) ** (NTERMS - 1) / (2 * NTERMS - 1)
    result = jnp.broadcast_to(identity * leading, curvature_gram.shape)
    for degree in range(NTERMS - 2, -1, -1):
        result = identity * ((-1.0) ** degree / (2 * degree + 1)) + jnp.matmul(curvature_gram, result, precision=HIGHEST_PRECISION)
    return result

def reference(bases, reference_basis, mass, interp_weights):
    inverse_rows = 1.0 / NROWS
    weighted = reference_basis * mass[:, None]

    def accumulate(summed, inputs):
        sampled, weight = inputs
        cross_gram = jnp.dot(weighted.T, sampled, precision=HIGHEST_PRECISION) * inverse_rows
        inverse = invert(cross_gram)
        shifted = jnp.dot(sampled, inverse, precision=HIGHEST_PRECISION) - reference_basis
        curvature_gram = jnp.dot((shifted * mass[:, None]).T, shifted, precision=HIGHEST_PRECISION) * inverse_rows
        factors = series(curvature_gram) * weight
        return (summed + jnp.dot(shifted, factors, precision=HIGHEST_PRECISION), None)
    summed, unused = lax.scan(accumulate, jnp.zeros((NROWS, R), jnp.float32), (bases, interp_weights))
    return summed
```

```python
import functools

import jax
import jax.numpy as jnp
from jax import lax
from jax.experimental import pallas as pl
from jax.experimental.pallas import tpu as pltpu
from jax.sharding import PartitionSpec as P

NTERMS = 6
MESH = pl.DeviceIdType.MESH
F32, BF16 = jnp.float32, jnp.bfloat16
HIGHEST = lax.Precision.HIGHEST
NN = (((1,), (0,)), ((), ()))
NT = (((1,), (1,)), ((), ()))
LEAF = 64


def split(x):
    high = x.astype(BF16)
    return high, (x - high.astype(F32)).astype(BF16)


def dot(a, b, dims=NN):
    return lax.dot_general(a, b, dims, preferred_element_type=F32)


def dot3(a, b, dims=NN):
    (ah, al), (bh, bl) = a, b
    return dot(ah, bh, dims) + (dot(ah, bl, dims) + dot(al, bh, dims))


def matmul(a, b):
    return dot3(split(a), split(b))


def exact(a, b, dims=NN):
    return lax.dot_general(a, b, dims, precision=HIGHEST, preferred_element_type=F32)


def pack(first, second):
    middle = jnp.concatenate([first[:, 128:], second[:, 128:]], axis=1)
    return jnp.concatenate([first[:, :128], middle, second[:, :128]], axis=1)


def unpack(packed):
    middle = packed[:, 128:256]
    half = middle.shape[1] // 2
    first = jnp.concatenate([packed[:, :128], middle[:, :half]], axis=1)
    second = jnp.concatenate([packed[:, 256:384], middle[:, half:]], axis=1)
    return first, second


def sweep_leaf(leaf_ref):
    lane = lax.broadcasted_iota(jnp.int32, (8, 128), 1)
    row = lax.broadcasted_iota(jnp.int32, (8, 128), 0)
    within = lane & (LEAF - 1)
    start = lane - within

    def step(p, carry):
        first = 8 * p
        index = [start + first + c for c in range(8)]
        own = pl.ds(pl.multiple_of(first, 8), 8)
        pivot = leaf_ref[own, :]

        def column(x, c):
            return jnp.take_along_axis(x, index[c], axis=1, mode="promise_in_bounds")

        columns = [column(pivot, c) for c in range(8)]
        e = {
            (r, c): jnp.broadcast_to(columns[c][r : r + 1, :], (8, 128))
            for c in range(8)
            for r in range(c + 1)
        }

        def at(r, c):
            return (r, c) if r <= c else (c, r)

        for k in range(8):
            inverse = 1.0 / e[k, k]
            scaled = {j: e[at(k, j)] * inverse for j in range(8) if j != k}
            for j in range(8):
                for i in range(j + 1):
                    if i != k and j != k:
                        e[i, j] = e[i, j] - e[at(i, k)] * scaled[j]
            for j in scaled:
                e[at(k, j)] = scaled[j]
            e[k, k] = -inverse

        inside = (within >= first) & (within < first + 8)
        rows = [
            jnp.where(
                within == first + c,
                1.0,
                jnp.where(inside, 0.0, -jnp.broadcast_to(pivot[c : c + 1, :], (8, 128))),
            )
            for c in range(8)
        ]
        scaled_rows = []
        for r in range(8):
            total = e[at(r, 0)] * rows[0]
            for c in range(1, 8):
                total = total + e[at(r, c)] * rows[c]
            scaled_rows.append(total)
        for g in range(LEAF // 8):
            block = leaf_ref[8 * g : 8 * g + 8, :]
            total = jnp.where(inside, 0.0, block)
            for c in range(8):
                total = total - column(block, c) * scaled_rows[c]
            leaf_ref[8 * g : 8 * g + 8, :] = total
        joined = scaled_rows[0]
        for r in range(1, 8):
            joined = jnp.where(row == r, scaled_rows[r], joined)
        leaf_ref[own, :] = joined
        return carry

    lax.fori_loop(0, LEAF // 8, step, 0)


def invert(normal, leaf_ref, between):
    size = normal[0].shape[0]
    row = lax.broadcasted_iota(jnp.int32, (LEAF, size), 0)
    lane = lax.broadcasted_iota(jnp.int32, (LEAF, size), 1)
    every_lane = lax.broadcasted_iota(jnp.int32, (size, size), 1)
    for i in range(size // LEAF):
        own = slice(LEAF * i, LEAF * (i + 1))
        leaf_ref[...] = jnp.concatenate([n[own, own] for n in normal], axis=1)
        sweep_leaf(leaf_ref)
        if i == 0:
            between()
        minus_inverse = leaf_ref[...]
        updated = []
        for s, n in enumerate(normal):
            panel = jnp.where(
                lane == row + LEAF * i, 1.0, jnp.where((lane >= LEAF * i) & (lane < LEAF * (i + 1)), 0.0, -n[own, :])
            )
            scaled = exact(minus_inverse[:, LEAF * s : LEAF * (s + 1)], panel)
            kept = jnp.where((every_lane >= LEAF * i) & (every_lane < LEAF * (i + 1)), 0.0, n)
            new = kept - exact(n[:, own], scaled)
            parts = [new[: LEAF * i], scaled, new[LEAF * (i + 1) :]]
            updated.append(jnp.concatenate([part for part in parts if part.shape[0]], axis=0))
        normal = updated
    return normal


def series(curvature):
    size = curvature.shape[0]
    diagonal = lax.broadcasted_iota(jnp.int32, (size, size), 0) == lax.broadcasted_iota(jnp.int32, (size, size), 1)
    weight = [(-1.0) ** n / (2 * n + 1) for n in range(NTERMS)]

    def pair(n):
        return weight[n + 1] * curvature + jnp.where(diagonal, weight[n], 0.0)

    pieces = split(curvature)
    square = split(dot3(pieces, pieces))
    result = pair(NTERMS - 2)
    for n in range(NTERMS - 4, -1, -2):
        result = pair(n) + dot3(square, split(result))
    return result


def kernel(
    cells,
    depth,
    samps,
    bases_ref,
    own_ref,
    mass_ref,
    weight_ref,
    out_ref,
    gathered,
    zh,
    zl,
    gram,
    curv,
    c_own,
    c_in,
    c_all,
    g_own,
    g_in,
    g_all,
    leaf,
    lhs_h,
    lhs_l,
    pair_out,
    pair_in,
    sums,
    far_in,
    near_in,
    gather_send,
    gather_left,
    gather_right,
    gather_far,
    gather_pair,
    reduce_send,
    reduce_recv,
    final_send,
    final_pair,
    final_far,
    final_near,
):
    size, block = own_ref.shape
    half = size // 2
    groups = size // 8
    cell = lax.axis_index("cell")
    samp = lax.axis_index("samp")
    chips = samps // 2
    core = lax.rem(samp, 2)
    y = samp // 2

    def there(step):
        return lax.rem(y + step + chips, chips)

    def slot(step, other=False):
        return 2 * there(step) + (1 - core if other else core)

    partner, right, left = slot(0, True), slot(1), slot(-1)

    barrier = pltpu.get_barrier_semaphore()

    def greet(d, carry):
        pl.semaphore_signal(barrier, inc=1, device_id={"cell": lax.rem(cell + d, cells)}, device_id_type=MESH)
        return carry

    lax.fori_loop(1, cells, greet, 0)
    for friend in (partner, right, left):
        pl.semaphore_signal(barrier, inc=1, device_id={"samp": friend}, device_id_type=MESH)
    pl.semaphore_wait(barrier, cells + 2)

    def send(src, dst, send_sem, recv_sem, to):
        copy = pltpu.make_async_remote_copy(
            src_ref=src,
            dst_ref=dst,
            send_sem=send_sem,
            recv_sem=recv_sem,
            device_id={"samp": to},
            device_id_type=MESH,
        )
        copy.start()
        return copy

    def arrived(ref, sem):
        pltpu.make_async_copy(ref, ref, sem).wait()

    def rows(h):
        return pl.ds(half * h, half)

    sent = []
    mine = gathered.at[samp]
    for h in (0, 1):
        sent.append(send(own_ref.at[rows(h)], mine.at[rows(h)], gather_send.at[h], gather_left.at[h], right))
        sent.append(send(own_ref.at[rows(1 - h)], mine.at[rows(1 - h)], gather_send.at[3 - h], gather_right.at[1 - h], left))
    sent.append(send(own_ref, mine, gather_send.at[4], gather_pair.at[0], partner))

    def weights(j):
        return mass_ref[:, pl.ds(pl.multiple_of(j * block, block), block)] * (1.0 / depth)

    def own_gram(j, carry):
        columns = pl.ds(pl.multiple_of(j * block, block), block)
        mass = weights(j)
        for s in range(2):
            x = bases_ref[s, :, columns]
            xh, xl = split(x)
            at = pl.ds(size * (s + 1), size)
            zh[j, at, :] = xh
            zl[j, at, :] = xl
            term = dot3((xh, xl), split(x * mass), NT)
            curv[s] = jnp.where(j == 0, term, curv[s] + term)
        return carry

    curv[...] = jnp.zeros_like(curv)
    lax.fori_loop(0, samps, own_gram, 0)

    def cross(j, x, first=False):
        xh, xl = split(x)
        zh[j, pl.ds(0, size), :] = xh
        zl[j, pl.ds(0, size), :] = xl
        term = dot3((zh[j], zl[j]), split(x * weights(j)), NT)
        if first:
            gram[...] = term
        else:
            gram[...] += term

    cross(samp, own_ref[...], True)

    arrived(mine.at[rows(0)], gather_left.at[0])
    from_left, from_right, far = gathered.at[left], gathered.at[right], gathered.at[slot(2)]
    sent.append(send(from_left.at[rows(0)], from_left.at[rows(0)], gather_send.at[5], gather_far.at[0], right))
    arrived(mine.at[rows(1)], gather_right.at[1])
    sent.append(send(from_right.at[rows(1)], from_right.at[rows(1)], gather_send.at[6], gather_far.at[1], left))
    arrived(mine.at[rows(1)], gather_left.at[1])
    sent.append(send(from_left, from_left, gather_send.at[7], gather_pair.at[1], partner))
    arrived(mine.at[rows(0)], gather_right.at[0])
    sent.append(send(from_right, from_right, gather_send.at[8], gather_pair.at[2], partner))
    arrived(mine, gather_pair.at[0])
    cross(partner, gathered[partner])
    cross(left, gathered[left])
    cross(right, gathered[right])
    arrived(mine.at[rows(0)], gather_far.at[0])
    arrived(mine.at[rows(1)], gather_far.at[1])
    sent.append(send(far, far, gather_send.at[9], gather_pair.at[3], partner))
    cross(slot(2), gathered[slot(2)])
    for i, step in ((1, -1), (2, 1), (3, 2)):
        arrived(mine, gather_pair.at[i])
        cross(slot(step, True), gathered[slot(step, True)])

    line = 8
    per_line = groups * line // cells

    class Reduction:
        def __init__(self, own, incoming, whole, sem, shift):
            self.own, self.incoming, self.whole, self.shift = own, incoming, whole, shift
            self.scatter_send, self.scatter_recv = reduce_send.at[sem], reduce_recv.at[sem]
            self.share_send, self.share_recv = reduce_send.at[sem + 1], reduce_recv.at[sem + 1]
            self.owns = self.is_owner(cell)

        def is_owner(self, c):
            z = lax.rem(c, line) - self.shift
            return (z >= 0) & (z < per_line)

        def group(self, c):
            return pl.ds(pl.multiple_of(8 * ((c // line) * per_line + lax.rem(c, line) - self.shift), 8), 8)

        def scatter(self):
            def one(d, carry):
                to = lax.rem(cell + d, cells)

                @pl.when(self.is_owner(to))
                def _():
                    pltpu.make_async_remote_copy(
                        src_ref=self.own.at[self.group(to)],
                        dst_ref=self.incoming.at[cell],
                        send_sem=self.scatter_send,
                        recv_sem=self.scatter_recv,
                        device_id={"cell": to},
                        device_id_type=MESH,
                    ).start()

                return carry

            lax.fori_loop(1, cells, one, 0)

        def share(self):
            @pl.when(self.owns)
            def _():
                self.incoming[cell] = self.own[self.group(cell), :]
                others = self.incoming.at[pl.ds(0, cells - 1)]
                arrived(others, self.scatter_recv)
                self.whole[self.group(cell), :] = jnp.sum(self.incoming[...], axis=0)

                def one(d, carry):
                    pltpu.make_async_remote_copy(
                        src_ref=self.whole.at[self.group(cell)],
                        dst_ref=self.whole.at[self.group(cell)],
                        send_sem=self.share_send,
                        recv_sem=self.share_recv,
                        device_id={"cell": lax.rem(cell + d, cells)},
                        device_id_type=MESH,
                    ).start()
                    return carry

                lax.fori_loop(1, cells, one, 0)

        def either(self, sem):
            @pl.when(self.owns)
            def _():
                arrived(self.own.at[pl.ds(0, size - 8)], sem)

            @pl.when(jnp.logical_not(self.owns))
            def _():
                arrived(self.own, sem)

        def finish(self):
            self.either(self.share_recv)

        def drain(self):
            self.either(self.scatter_send)

            @pl.when(self.owns)
            def _():
                arrived(self.incoming.at[pl.ds(0, cells - 1)], self.share_send)

    reduce_c = Reduction(c_own, c_in, c_all, 0, 0)
    reduce_g = Reduction(g_own, g_in, g_all, 2, line - per_line)

    c_own[...] = pack(gram[size : 2 * size], gram[2 * size :])
    reduce_c.scatter()
    g_own[:, :384] = pack(curv[0], curv[1])
    g_own[:, 384:] = gram[:size]
    reduce_g.scatter()
    reduce_c.share()
    reduce_c.finish()

    cross_t = unpack(c_all[...])
    normal = [exact(c, c, NT) for c in cross_t]
    minus_inverse = invert(normal, leaf, reduce_g.share)
    inverses = [-exact(m, c) for m, c in zip(minus_inverse, cross_t)]

    reduce_g.finish()
    of_bases = unpack(g_all[:, :384])
    of_reference = g_all[:, 384:]
    plain = jnp.zeros((size, size), F32)
    for s in range(2):
        x = split(inverses[s])
        turned = inverses[s].T
        middle = dot3(split(of_bases[s]), x) - 2.0 * cross_t[s]
        curvature = matmul(turned, middle) + of_reference
        factors = series(curvature) * weight_ref[s]
        plain = plain - factors
        lhs_h[s + 1], lhs_l[s + 1] = split(matmul(factors, turned))
    lhs_h[0], lhs_l[0] = split(plain)

    def term(j):
        total = None
        for k in range(3):
            at = pl.ds(size * k, size)
            part = dot3((lhs_h[k], lhs_l[k]), (zh[j, at, :], zl[j, at, :]))
            total = part if total is None else total + part
        return total

    steps = (2, 1, -1, 0)
    for i, step in enumerate(steps):
        pair_out[i] = term(slot(step, True))
        sent.append(send(pair_out.at[i], pair_in.at[i], final_send.at[i], final_pair.at[i], partner))

    def own_term(i):
        value = term(slot(steps[i]))
        arrived(pair_in.at[i], final_pair.at[i])
        return value + pair_in[i]

    def forward(i, h, to, sem, recv, dst):
        sent.append(send(sums.at[i, rows(h)], dst, final_send.at[sem], recv, to))

    sums[0] = own_term(0)
    forward(0, 0, right, 4, final_far.at[0], far_in.at[0])
    forward(0, 1, left, 5, final_far.at[1], far_in.at[1])
    sums[1] = own_term(1)
    forward(1, 1, right, 6, final_near.at[1], near_in.at[0, rows(1)])
    sums[2] = own_term(2)
    forward(2, 0, left, 7, final_near.at[2], near_in.at[1, rows(0)])
    arrived(far_in.at[0], final_far.at[0])
    sums[1, rows(0), :] += far_in[0]
    forward(1, 0, right, 8, final_near.at[0], near_in.at[0, rows(0)])
    arrived(far_in.at[1], final_far.at[1])
    sums[2, rows(1), :] += far_in[1]
    forward(2, 1, left, 9, final_near.at[3], near_in.at[1, rows(1)])
    out_ref[...] = own_term(3)
    for i in range(4):
        arrived(far_in.at[0], final_near.at[i])
    out_ref[...] += near_in[0] + near_in[1]

    for copy in sent:
        copy.wait_send()
    reduce_c.drain()
    reduce_g.drain()


def body(bases, reference_basis, mass, interp_weights):
    cells, samps = lax.axis_size("cell"), lax.axis_size("samp")
    count, depth, size = bases.shape
    block = reference_basis.shape[0]
    packed, wide = 2 * size, 3 * size
    half = size // 2
    vmem = pl.BlockSpec(memory_space=pltpu.VMEM)
    result = pl.pallas_call(
        functools.partial(kernel, cells, depth * cells, samps),
        out_shape=jax.ShapeDtypeStruct((size, block), F32),
        in_specs=[vmem, vmem, vmem, pl.BlockSpec(memory_space=pltpu.SMEM)],
        out_specs=vmem,
        scratch_shapes=[
            pltpu.VMEM((samps, size, block), F32),
            pltpu.VMEM((samps, 3 * size, block), BF16),
            pltpu.VMEM((samps, 3 * size, block), BF16),
            pltpu.VMEM((3 * size, size), F32),
            pltpu.VMEM((2, size, size), F32),
            pltpu.VMEM((size, packed), F32),
            pltpu.VMEM((cells, 8, packed), F32),
            pltpu.VMEM((size, packed), F32),
            pltpu.VMEM((size, wide), F32),
            pltpu.VMEM((cells, 8, wide), F32),
            pltpu.VMEM((size, wide), F32),
            pltpu.VMEM((LEAF, 2 * LEAF), F32),
            pltpu.VMEM((3, size, size), BF16),
            pltpu.VMEM((3, size, size), BF16),
            pltpu.VMEM((4, size, block), F32),
            pltpu.VMEM((4, size, block), F32),
            pltpu.VMEM((3, size, block), F32),
            pltpu.VMEM((2, half, block), F32),
            pltpu.VMEM((2, size, block), F32),
            pltpu.SemaphoreType.DMA((10,)),
            pltpu.SemaphoreType.DMA((2,)),
            pltpu.SemaphoreType.DMA((2,)),
            pltpu.SemaphoreType.DMA((2,)),
            pltpu.SemaphoreType.DMA((4,)),
            pltpu.SemaphoreType.DMA((4,)),
            pltpu.SemaphoreType.DMA((4,)),
            pltpu.SemaphoreType.DMA((10,)),
            pltpu.SemaphoreType.DMA((4,)),
            pltpu.SemaphoreType.DMA((2,)),
            pltpu.SemaphoreType.DMA((4,)),
        ],
        compiler_params=pltpu.CompilerParams(
            collective_id=0, has_side_effects=True, vmem_limit_bytes=48 * 1024 * 1024
        ),
    )(jnp.swapaxes(bases, 1, 2), reference_basis.T, mass[None, :], interp_weights)
    return result.T


def solution(mesh):
    placed = (P("samp", "cell", None), P(("cell", "samp"), None), P("cell"), P("samp"))
    return jax.shard_map(
        body, mesh=mesh, in_specs=placed, out_specs=P(("cell", "samp"), None), check_vma=False
    )
```

```python
import functools

import jax
import jax.numpy as jnp
from jax import lax
from jax.experimental import pallas as pl
from jax.experimental.pallas import tpu as pltpu
from jax.sharding import PartitionSpec as P

NTERMS = 6
MESH = pl.DeviceIdType.MESH
F32, BF16 = jnp.float32, jnp.bfloat16
HIGHEST = lax.Precision.HIGHEST
NN = (((1,), (0,)), ((), ()))
NT = (((1,), (1,)), ((), ()))
LEAF = 64


def split(x):
    high = x.astype(BF16)
    return high, (x - high.astype(F32)).astype(BF16)


def dot(a, b, dims=NN):
    return lax.dot_general(a, b, dims, preferred_element_type=F32)


def dot3(a, b, dims=NN):
    (ah, al), (bh, bl) = a, b
    return dot(ah, bh, dims) + (dot(ah, bl, dims) + dot(al, bh, dims))


def matmul(a, b):
    return dot3(split(a), split(b))


def exact(a, b, dims=NN):
    return lax.dot_general(a, b, dims, precision=HIGHEST, preferred_element_type=F32)


def pack(first, second):
    middle = jnp.concatenate([first[:, 128:], second[:, 128:]], axis=1)
    return jnp.concatenate([first[:, :128], middle, second[:, :128]], axis=1)


def unpack(packed):
    middle = packed[:, 128:256]
    half = middle.shape[1] // 2
    first = jnp.concatenate([packed[:, :128], middle[:, :half]], axis=1)
    second = jnp.concatenate([packed[:, 256:384], middle[:, half:]], axis=1)
    return first, second


def sweep_leaf(leaf_ref):
    lane = lax.broadcasted_iota(jnp.int32, (8, 128), 1)
    row = lax.broadcasted_iota(jnp.int32, (8, 128), 0)
    within = lane & (LEAF - 1)
    start = lane - within

    def step(p, carry):
        first = 8 * p
        index = [start + first + c for c in range(8)]
        own = pl.ds(pl.multiple_of(first, 8), 8)
        pivot = leaf_ref[own, :]

        def column(x, c):
            return jnp.take_along_axis(x, index[c], axis=1, mode="promise_in_bounds")

        columns = [column(pivot, c) for c in range(8)]
        e = {
            (r, c): jnp.broadcast_to(columns[c][r : r + 1, :], (8, 128))
            for c in range(8)
            for r in range(c + 1)
        }

        def at(r, c):
            return (r, c) if r <= c else (c, r)

        for k in range(8):
            inverse = 1.0 / e[k, k]
            scaled = {j: e[at(k, j)] * inverse for j in range(8) if j != k}
            for j in range(8):
                for i in range(j + 1):
                    if i != k and j != k:
                        e[i, j] = e[i, j] - e[at(i, k)] * scaled[j]
            for j in scaled:
                e[at(k, j)] = scaled[j]
            e[k, k] = -inverse

        inside = (within >= first) & (within < first + 8)
        rows = [
            jnp.where(
                within == first + c,
                1.0,
                jnp.where(inside, 0.0, -jnp.broadcast_to(pivot[c : c + 1, :], (8, 128))),
            )
            for c in range(8)
        ]
        scaled_rows = []
        for r in range(8):
            total = e[at(r, 0)] * rows[0]
            for c in range(1, 8):
                total = total + e[at(r, c)] * rows[c]
            scaled_rows.append(total)
        for g in range(LEAF // 8):
            block = leaf_ref[8 * g : 8 * g + 8, :]
            total = jnp.where(inside, 0.0, block)
            for c in range(8):
                total = total - column(block, c) * scaled_rows[c]
            leaf_ref[8 * g : 8 * g + 8, :] = total
        joined = scaled_rows[0]
        for r in range(1, 8):
            joined = jnp.where(row == r, scaled_rows[r], joined)
        leaf_ref[own, :] = joined
        return carry

    lax.fori_loop(0, LEAF // 8, step, 0)


def invert(normal, leaf_ref, between):
    size = normal[0].shape[0]
    row = lax.broadcasted_iota(jnp.int32, (LEAF, size), 0)
    lane = lax.broadcasted_iota(jnp.int32, (LEAF, size), 1)
    every_lane = lax.broadcasted_iota(jnp.int32, (size, size), 1)
    for i in range(size // LEAF):
        own = slice(LEAF * i, LEAF * (i + 1))
        leaf_ref[...] = jnp.concatenate([n[own, own] for n in normal], axis=1)
        sweep_leaf(leaf_ref)
        if i == 0:
            between()
        minus_inverse = leaf_ref[...]
        updated = []
        for s, n in enumerate(normal):
            panel = jnp.where(
                lane == row + LEAF * i, 1.0, jnp.where((lane >= LEAF * i) & (lane < LEAF * (i + 1)), 0.0, -n[own, :])
            )
            scaled = exact(minus_inverse[:, LEAF * s : LEAF * (s + 1)], panel)
            kept = jnp.where((every_lane >= LEAF * i) & (every_lane < LEAF * (i + 1)), 0.0, n)
            new = kept - exact(n[:, own], scaled)
            parts = [new[: LEAF * i], scaled, new[LEAF * (i + 1) :]]
            updated.append(jnp.concatenate([part for part in parts if part.shape[0]], axis=0))
        normal = updated
    return normal


def series(curvature):
    size = curvature.shape[0]
    diagonal = lax.broadcasted_iota(jnp.int32, (size, size), 0) == lax.broadcasted_iota(jnp.int32, (size, size), 1)
    weight = [(-1.0) ** n / (2 * n + 1) for n in range(NTERMS)]

    def pair(n):
        return weight[n + 1] * curvature + jnp.where(diagonal, weight[n], 0.0)

    pieces = split(curvature)
    square = split(dot3(pieces, pieces))
    result = pair(NTERMS - 2)
    for n in range(NTERMS - 4, -1, -2):
        result = pair(n) + dot3(square, split(result))
    return result


def kernel(
    cells,
    depth,
    samps,
    bases_hbm,
    own_hbm,
    mass_hbm,
    weight_hbm,
    out_ref,
    bases,
    mass_row,
    weight_ref,
    gathered,
    zh,
    zl,
    gram,
    curv,
    c_own,
    c_in,
    c_all,
    g_own,
    g_x,
    g_part,
    g_z,
    h_in,
    g_all,
    leaf,
    lhs_h,
    lhs_l,
    pair_out,
    pair_in,
    sums,
    far_in,
    near_in,
    load_sem,
    gather_send,
    gather_left,
    gather_right,
    gather_far,
    gather_pair,
    reduce_send,
    reduce_recv,
    final_send,
    final_pair,
    final_far,
    final_near,
):
    size, block = own_hbm.shape
    half = size // 2
    cell = lax.axis_index("cell")
    samp = lax.axis_index("samp")
    chips = samps // 2
    core = lax.rem(samp, 2)
    y = samp // 2
    line = 8
    lines = cells // line
    x, z = cell // line, lax.rem(cell, line)

    def there(step):
        return lax.rem(y + step + chips, chips)

    def slot(step, other=False):
        return 2 * there(step) + (1 - core if other else core)

    partner, right, left = slot(0, True), slot(1), slot(-1)

    def other_cell(d):
        return lax.rem(cell + d, cells)

    def other_samp(d):
        return lax.rem(samp + d, samps)

    barrier = pltpu.get_barrier_semaphore()
    for d in range(1, samps):
        pl.semaphore_signal(barrier, inc=1, device_id={"samp": other_samp(d)}, device_id_type=MESH)
    for d in range(1, cells):
        pl.semaphore_signal(barrier, inc=1, device_id={"cell": other_cell(d)}, device_id_type=MESH)

    def columns(j):
        return pl.ds(pl.multiple_of(j * block, block), block)

    def load_bases(j):
        at = bases.at[:, :, columns(j)]
        return pltpu.make_async_copy(bases_hbm.at[:, :, columns(j)], at, load_sem.at[j])

    loads = [
        pltpu.make_async_copy(mass_hbm, mass_row, load_sem.at[samps]),
        pltpu.make_async_copy(own_hbm, gathered.at[samp], load_sem.at[samps + 1]),
        pltpu.make_async_copy(weight_hbm, weight_ref, load_sem.at[samps + 2]),
    ]
    for load in loads:
        load.start()
    for j in range(samps):
        load_bases(j).start()

    def weights(j):
        return mass_row[:, columns(j)] * (1.0 / depth)

    for load in loads:
        load.wait()
    mine = gathered.at[samp]
    reference = mine[...]
    g_own[:, 2 * size :] = dot3(split(reference), split(reference * weights(samp)), NT)

    def own_gram(j, carry):
        load_bases(j).wait()
        mass = weights(j)
        for s in range(2):
            value = bases[s, :, columns(j)]
            high, low = split(value)
            at = pl.ds(size * (s + 1), size)
            zh[j, at, :] = high
            zl[j, at, :] = low
            curv[s] += dot3((high, low), split(value * mass), NT)
        return carry

    curv[...] = jnp.zeros_like(curv)
    lax.fori_loop(0, samps, own_gram, 0)
    g_own[:, : 2 * size] = pack(curv[0], curv[1])

    def cross(j, first=False):
        value = gathered[j]
        high, low = split(value)
        zh[j, pl.ds(0, size), :] = high
        zl[j, pl.ds(0, size), :] = low
        at = pl.ds(size, 2 * size)
        term = dot3((zh[j, at, :], zl[j, at, :]), split(value * weights(j)), NT)
        if first:
            gram[...] = term
        else:
            gram[...] += term

    cross(samp, True)

    pl.semaphore_wait(barrier, cells + samps - 2)

    def remote(src, dst, send_sem, recv_sem, **to):
        copy = pltpu.make_async_remote_copy(
            src_ref=src, dst_ref=dst, send_sem=send_sem, recv_sem=recv_sem, device_id=to, device_id_type=MESH
        )
        copy.start()
        return copy

    def send(src, dst, send_sem, recv_sem, to):
        return remote(src, dst, send_sem, recv_sem, samp=to)

    def arrived(ref, sem):
        pltpu.make_async_copy(ref, ref, sem).wait()

    def rows(h):
        return pl.ds(half * h, half)

    sent = []
    for h in (0, 1):
        sent.append(send(mine.at[rows(h)], mine.at[rows(h)], gather_send.at[h], gather_left.at[h], right))
        sent.append(send(mine.at[rows(1 - h)], mine.at[rows(1 - h)], gather_send.at[3 - h], gather_right.at[1 - h], left))
    sent.append(send(mine, mine, gather_send.at[4], gather_pair.at[0], partner))

    quarter = size // lines
    owns_g = z < quarter // 8

    def g_rows(x_of, z_of=None):
        if z_of is None:
            return pl.ds(pl.multiple_of(quarter * x_of, 8), quarter)
        return pl.ds(pl.multiple_of(quarter * x_of + 8 * z_of, 8), 8)

    def count_rows(n):
        return g_own.at[pl.ds(0, n)]

    def g_scatter_x():
        for d in range(1, lines):
            to = lax.rem(x + d, lines)
            remote(g_own.at[g_rows(to)], g_x.at[x], reduce_send.at[0], reduce_recv.at[0], cell=to * line + z)

    def g_scatter_z():
        g_x[x] = g_own[g_rows(x), :]
        arrived(count_rows(quarter * (lines - 1)), reduce_recv.at[0])
        g_part[...] = jnp.sum(g_x[...], axis=0)
        for d in range(1, line):
            to = lax.rem(z + d, line)

            @pl.when(to < quarter // 8)
            def _(to=to):
                src = g_part.at[pl.ds(pl.multiple_of(8 * to, 8), 8)]
                remote(src, g_z.at[z], reduce_send.at[1], reduce_recv.at[1], cell=x * line + to)

    def g_scatter_samp():
        @pl.when(owns_g)
        def _():
            g_z[z] = g_part[pl.ds(pl.multiple_of(8 * z, 8), 8), :]
            arrived(count_rows(8 * (line - 1)), reduce_recv.at[1])
            total = jnp.sum(g_z[...], axis=0)
            g_all[g_rows(x, z), : 2 * size] = total[:, : 2 * size]
            h_in[samp] = total[:, 2 * size :]
            for d in range(1, samps):
                remote(h_in.at[samp], h_in.at[samp], reduce_send.at[2], reduce_recv.at[2], samp=other_samp(d))

    def g_share_z():
        @pl.when(owns_g)
        def _():
            arrived(h_in.at[pl.ds(0, samps - 1)], reduce_recv.at[2])
            g_all[g_rows(x, z), 2 * size :] = jnp.sum(h_in[...], axis=0)
            piece = g_all.at[g_rows(x, z)]
            for d in range(1, line):
                to = lax.rem(z + d, line)
                remote(piece, piece, reduce_send.at[3], reduce_recv.at[3], cell=x * line + to)

    def g_counted(owner, rest, sem):
        @pl.when(owns_g)
        def _():
            arrived(count_rows(owner), sem)

        if rest:

            @pl.when(jnp.logical_not(owns_g))
            def _():
                arrived(count_rows(rest), sem)

    def g_share_x():
        g_counted(quarter - 8, quarter, reduce_recv.at[3])
        piece = g_all.at[g_rows(x)]
        for d in range(1, lines):
            to = lax.rem(x + d, lines)
            remote(piece, piece, reduce_send.at[4], reduce_recv.at[4], cell=to * line + z)

    def g_finish():
        arrived(count_rows(quarter * (lines - 1)), reduce_recv.at[4])

    def g_drain():
        arrived(count_rows(quarter * (lines - 1)), reduce_send.at[0])
        g_counted(quarter - 8, quarter, reduce_send.at[1])

        @pl.when(owns_g)
        def _():
            arrived(h_in.at[pl.ds(0, samps - 1)], reduce_send.at[2])

        g_counted(8 * (line - 1), 0, reduce_send.at[3])
        arrived(count_rows(quarter * (lines - 1)), reduce_send.at[4])

    group = 16
    per_line = size // group // lines
    z_pair = z // 2
    owns_c = (lax.rem(z, 2) == lax.rem(x + core, 2)) & (z_pair < per_line)

    def c_rows(x_of, pair_of):
        return pl.ds(pl.multiple_of(group * (per_line * x_of + pair_of), group), group)

    def c_scatter():
        for dx in range(lines):
            to_x = lax.rem(x + dx, lines)
            for dq in range(per_line):
                to_pair = lax.rem(z_pair + dq, per_line)
                to = to_x * line + 2 * to_pair + lax.rem(to_x + core, 2)

                def one(to=to, to_x=to_x, to_pair=to_pair):
                    src = c_own.at[c_rows(to_x, to_pair)]
                    remote(src, c_in.at[cell], reduce_send.at[5], reduce_recv.at[5], cell=to)

                if dx:
                    one()
                else:
                    pl.when(to != cell)(one)

    def c_share():
        @pl.when(owns_c)
        def _():
            here = c_rows(x, z_pair)
            c_in[cell] = c_own[here, :]
            arrived(c_in.at[pl.ds(0, cells - 1)], reduce_recv.at[5])
            c_all[here, :] = jnp.sum(c_in[...], axis=0)
            for d in range(1, cells):
                remote(c_all.at[here], c_all.at[here], reduce_send.at[6], reduce_recv.at[6], cell=other_cell(d))

    def c_counted(sem):
        @pl.when(owns_c)
        def _():
            arrived(c_own.at[pl.ds(0, size - group)], sem)

        @pl.when(jnp.logical_not(owns_c))
        def _():
            arrived(c_own, sem)

    def c_drain():
        c_counted(reduce_send.at[5])

        @pl.when(owns_c)
        def _():
            arrived(c_in.at[pl.ds(0, cells - 1)], reduce_send.at[6])

    g_scatter_x()
    arrived(mine.at[rows(0)], gather_left.at[0])
    from_left, from_right, far = gathered.at[left], gathered.at[right], gathered.at[slot(2)]
    sent.append(send(from_left.at[rows(0)], from_left.at[rows(0)], gather_send.at[5], gather_far.at[0], right))
    arrived(mine.at[rows(1)], gather_right.at[1])
    sent.append(send(from_right.at[rows(1)], from_right.at[rows(1)], gather_send.at[6], gather_far.at[1], left))
    arrived(mine.at[rows(1)], gather_left.at[1])
    sent.append(send(from_left, from_left, gather_send.at[7], gather_pair.at[1], partner))
    arrived(mine.at[rows(0)], gather_right.at[0])
    sent.append(send(from_right, from_right, gather_send.at[8], gather_pair.at[2], partner))
    arrived(mine, gather_pair.at[0])
    cross(partner)
    cross(left)
    cross(right)
    g_scatter_z()
    arrived(mine.at[rows(0)], gather_far.at[0])
    arrived(mine.at[rows(1)], gather_far.at[1])
    sent.append(send(far, far, gather_send.at[9], gather_pair.at[3], partner))
    cross(slot(2))
    for i, step in ((1, -1), (2, 1), (3, 2)):
        arrived(mine, gather_pair.at[i])
        cross(slot(step, True))

    c_own[...] = pack(gram[:size], gram[size:])
    c_scatter()
    g_scatter_samp()
    c_share()
    g_share_z()
    c_counted(reduce_recv.at[6])

    cross_t = unpack(c_all[...])
    normal = [exact(c, c, NT) for c in cross_t]
    minus_inverse = invert(normal, leaf, g_share_x)
    inverses = [-exact(m, c) for m, c in zip(minus_inverse, cross_t)]

    g_finish()
    of_bases = unpack(g_all[:, : 2 * size])
    of_reference = g_all[:, 2 * size :]
    plain = jnp.zeros((size, size), F32)
    for s in range(2):
        inverse = split(inverses[s])
        turned = inverses[s].T
        middle = dot3(split(of_bases[s]), inverse) - 2.0 * cross_t[s]
        curvature = matmul(turned, middle) + of_reference
        factors = series(curvature) * weight_ref[s]
        plain = plain - factors
        lhs_h[s + 1], lhs_l[s + 1] = split(matmul(factors, turned))
    lhs_h[0], lhs_l[0] = split(plain)

    def term(j):
        total = None
        for k in range(3):
            at = pl.ds(size * k, size)
            part = dot3((lhs_h[k], lhs_l[k]), (zh[j, at, :], zl[j, at, :]))
            total = part if total is None else total + part
        return total

    steps = (2, 1, -1, 0)
    for i, step in enumerate(steps):
        pair_out[i] = term(slot(step, True))
        sent.append(send(pair_out.at[i], pair_in.at[i], final_send.at[i], final_pair.at[i], partner))

    def own_term(i):
        value = term(slot(steps[i]))
        arrived(pair_in.at[i], final_pair.at[i])
        return value + pair_in[i]

    def forward(i, h, to, sem, recv, dst):
        sent.append(send(sums.at[i, rows(h)], dst, final_send.at[sem], recv, to))

    sums[0] = own_term(0)
    forward(0, 0, right, 4, final_far.at[0], far_in.at[0])
    forward(0, 1, left, 5, final_far.at[1], far_in.at[1])
    sums[1] = own_term(1)
    forward(1, 1, right, 6, final_near.at[1], near_in.at[0, rows(1)])
    sums[2] = own_term(2)
    forward(2, 0, left, 7, final_near.at[2], near_in.at[1, rows(0)])
    arrived(far_in.at[0], final_far.at[0])
    sums[1, rows(0), :] += far_in[0]
    forward(1, 0, right, 8, final_near.at[0], near_in.at[0, rows(0)])
    arrived(far_in.at[1], final_far.at[1])
    sums[2, rows(1), :] += far_in[1]
    forward(2, 1, left, 9, final_near.at[3], near_in.at[1, rows(1)])
    out_ref[...] = own_term(3)
    for i in range(4):
        arrived(far_in.at[0], final_near.at[i])
    out_ref[...] += near_in[0] + near_in[1]

    for copy in sent:
        copy.wait_send()
    c_drain()
    g_drain()


def body(bases, reference_basis, mass, interp_weights):
    cells, samps = lax.axis_size("cell"), lax.axis_size("samp")
    count, depth, size = bases.shape
    block = reference_basis.shape[0]
    packed, wide = 2 * size, 3 * size
    half = size // 2
    hbm, vmem = pl.BlockSpec(memory_space=pltpu.HBM), pl.BlockSpec(memory_space=pltpu.VMEM)
    line, group = 8, 16
    lines = cells // line
    result = pl.pallas_call(
        functools.partial(kernel, cells, depth * cells, samps),
        out_shape=jax.ShapeDtypeStruct((size, block), F32),
        in_specs=[hbm] * 4,
        out_specs=vmem,
        scratch_shapes=[
            pltpu.VMEM((count, size, depth), F32),
            pltpu.VMEM((1, depth), F32),
            pltpu.SMEM((count,), F32),
            pltpu.VMEM((samps, size, block), F32),
            pltpu.VMEM((samps, 3 * size, block), BF16),
            pltpu.VMEM((samps, 3 * size, block), BF16),
            pltpu.VMEM((packed, size), F32),
            pltpu.VMEM((2, size, size), F32),
            pltpu.VMEM((size, packed), F32),
            pltpu.VMEM((cells, group, packed), F32),
            pltpu.VMEM((size, packed), F32),
            pltpu.VMEM((size, wide), F32),
            pltpu.VMEM((lines, size // lines, wide), F32),
            pltpu.VMEM((size // lines, wide), F32),
            pltpu.VMEM((line, 8, wide), F32),
            pltpu.VMEM((samps, 8, size), F32),
            pltpu.VMEM((size, wide), F32),
            pltpu.VMEM((LEAF, 2 * LEAF), F32),
            pltpu.VMEM((3, size, size), BF16),
            pltpu.VMEM((3, size, size), BF16),
            pltpu.VMEM((4, size, block), F32),
            pltpu.VMEM((4, size, block), F32),
            pltpu.VMEM((3, size, block), F32),
            pltpu.VMEM((2, half, block), F32),
            pltpu.VMEM((2, size, block), F32),
            pltpu.SemaphoreType.DMA((samps + 3,)),
            pltpu.SemaphoreType.DMA((10,)),
            pltpu.SemaphoreType.DMA((2,)),
            pltpu.SemaphoreType.DMA((2,)),
            pltpu.SemaphoreType.DMA((2,)),
            pltpu.SemaphoreType.DMA((4,)),
            pltpu.SemaphoreType.DMA((7,)),
            pltpu.SemaphoreType.DMA((7,)),
            pltpu.SemaphoreType.DMA((10,)),
            pltpu.SemaphoreType.DMA((4,)),
            pltpu.SemaphoreType.DMA((2,)),
            pltpu.SemaphoreType.DMA((4,)),
        ],
        compiler_params=pltpu.CompilerParams(
            collective_id=0, has_side_effects=True, vmem_limit_bytes=48 * 1024 * 1024
        ),
    )(jnp.swapaxes(bases, 1, 2), reference_basis.T, mass[None, :], interp_weights)
    return result.T


def solution(mesh):
    placed = (P("samp", "cell", None), P(("cell", "samp"), None), P("cell"), P("samp"))
    return jax.shard_map(
        body, mesh=mesh, in_specs=placed, out_specs=P(("cell", "samp"), None), check_vma=False
    )
```

```python
import functools

import jax
import jax.numpy as jnp
from jax import lax
from jax.experimental import pallas as pl
from jax.experimental.pallas import tpu as pltpu
from jax.sharding import PartitionSpec as P

NTERMS = 6
MESH = pl.DeviceIdType.MESH
F32, BF16 = jnp.float32, jnp.bfloat16
HIGHEST = lax.Precision.HIGHEST
NN = (((1,), (0,)), ((), ()))
NT = (((1,), (1,)), ((), ()))
LEAF = 64


def split(x):
    high = x.astype(BF16)
    return high, (x - high.astype(F32)).astype(BF16)


def dot(a, b, dims=NN):
    return lax.dot_general(a, b, dims, preferred_element_type=F32)


def dot3(a, b, dims=NN):
    (ah, al), (bh, bl) = a, b
    return dot(ah, bh, dims) + (dot(ah, bl, dims) + dot(al, bh, dims))


def matmul(a, b):
    return dot3(split(a), split(b))


def exact(a, b, dims=NN):
    return lax.dot_general(a, b, dims, precision=HIGHEST, preferred_element_type=F32)


def pack(first, second):
    middle = jnp.concatenate([first[:, 128:], second[:, 128:]], axis=1)
    return jnp.concatenate([first[:, :128], middle, second[:, :128]], axis=1)


def unpack(packed):
    middle = packed[:, 128:256]
    half = middle.shape[1] // 2
    first = jnp.concatenate([packed[:, :128], middle[:, :half]], axis=1)
    second = jnp.concatenate([packed[:, 256:384], middle[:, half:]], axis=1)
    return first, second


def sweep_leaf(leaf_ref):
    lane = lax.broadcasted_iota(jnp.int32, (8, 128), 1)
    row = lax.broadcasted_iota(jnp.int32, (8, 128), 0)
    within = lane & (LEAF - 1)
    start = lane - within

    def step(p, carry):
        first = 8 * p
        index = [start + first + c for c in range(8)]
        own = pl.ds(pl.multiple_of(first, 8), 8)
        pivot = leaf_ref[own, :]

        def column(x, c):
            return jnp.take_along_axis(x, index[c], axis=1, mode="promise_in_bounds")

        columns = [column(pivot, c) for c in range(8)]
        e = {
            (r, c): jnp.broadcast_to(columns[c][r : r + 1, :], (8, 128))
            for c in range(8)
            for r in range(c + 1)
        }

        def at(r, c):
            return (r, c) if r <= c else (c, r)

        for k in range(8):
            inverse = 1.0 / e[k, k]
            scaled = {j: e[at(k, j)] * inverse for j in range(8) if j != k}
            for j in range(8):
                for i in range(j + 1):
                    if i != k and j != k:
                        e[i, j] = e[i, j] - e[at(i, k)] * scaled[j]
            for j in scaled:
                e[at(k, j)] = scaled[j]
            e[k, k] = -inverse

        inside = (within >= first) & (within < first + 8)
        rows = [
            jnp.where(
                within == first + c,
                1.0,
                jnp.where(inside, 0.0, -jnp.broadcast_to(pivot[c : c + 1, :], (8, 128))),
            )
            for c in range(8)
        ]
        scaled_rows = []
        for r in range(8):
            total = e[at(r, 0)] * rows[0]
            for c in range(1, 8):
                total = total + e[at(r, c)] * rows[c]
            scaled_rows.append(total)
        for g in range(LEAF // 8):
            block = leaf_ref[8 * g : 8 * g + 8, :]
            total = jnp.where(inside, 0.0, block)
            for c in range(8):
                total = total - column(block, c) * scaled_rows[c]
            leaf_ref[8 * g : 8 * g + 8, :] = total
        joined = scaled_rows[0]
        for r in range(1, 8):
            joined = jnp.where(row == r, scaled_rows[r], joined)
        leaf_ref[own, :] = joined
        return carry

    lax.fori_loop(0, LEAF // 8, step, 0)


def invert(normal, leaf_ref, between):
    size = normal[0].shape[0]
    row = lax.broadcasted_iota(jnp.int32, (LEAF, size), 0)
    lane = lax.broadcasted_iota(jnp.int32, (LEAF, size), 1)
    every_lane = lax.broadcasted_iota(jnp.int32, (size, size), 1)
    for i in range(size // LEAF):
        own = slice(LEAF * i, LEAF * (i + 1))
        leaf_ref[...] = jnp.concatenate([n[own, own] for n in normal], axis=1)
        sweep_leaf(leaf_ref)
        if i == 0:
            between()
        minus_inverse = leaf_ref[...]
        updated = []
        for s, n in enumerate(normal):
            panel = jnp.where(
                lane == row + LEAF * i, 1.0, jnp.where((lane >= LEAF * i) & (lane < LEAF * (i + 1)), 0.0, -n[own, :])
            )
            scaled = exact(minus_inverse[:, LEAF * s : LEAF * (s + 1)], panel)
            kept = jnp.where((every_lane >= LEAF * i) & (every_lane < LEAF * (i + 1)), 0.0, n)
            new = kept - exact(n[:, own], scaled)
            parts = [new[: LEAF * i], scaled, new[LEAF * (i + 1) :]]
            updated.append(jnp.concatenate([part for part in parts if part.shape[0]], axis=0))
        normal = updated
    return normal


def series(curvature):
    size = curvature.shape[0]
    diagonal = lax.broadcasted_iota(jnp.int32, (size, size), 0) == lax.broadcasted_iota(jnp.int32, (size, size), 1)
    weight = [(-1.0) ** n / (2 * n + 1) for n in range(NTERMS)]

    def pair(n):
        return weight[n + 1] * curvature + jnp.where(diagonal, weight[n], 0.0)

    pieces = split(curvature)
    square = split(dot3(pieces, pieces))
    result = pair(NTERMS - 2)
    for n in range(NTERMS - 4, -1, -2):
        result = pair(n) + dot3(square, split(result))
    return result


def kernel(
    cells,
    depth,
    samps,
    bases_hbm,
    own_hbm,
    mass_hbm,
    weight_hbm,
    out_ref,
    bases,
    mass_row,
    weight_ref,
    gathered,
    zh,
    zl,
    gram,
    curv,
    c_x,
    c_part,
    c_z,
    c_all,
    g_own,
    g_x,
    g_part,
    g_z,
    h_in,
    g_all,
    leaf,
    lhs_h,
    lhs_l,
    pair_out,
    pair_in,
    sums,
    far_in,
    near_in,
    load_sem,
    gather_send,
    gather_left,
    gather_right,
    gather_far,
    gather_pair,
    reduce_send,
    reduce_recv,
    final_send,
    final_pair,
    final_far,
    final_near,
):
    size, block = own_hbm.shape
    half = size // 2
    cell = lax.axis_index("cell")
    samp = lax.axis_index("samp")
    chips = samps // 2
    core = lax.rem(samp, 2)
    y = samp // 2
    line = 8
    lines = cells // line
    x, z = cell // line, lax.rem(cell, line)

    def there(step):
        return lax.rem(y + step + chips, chips)

    def slot(step, other=False):
        return 2 * there(step) + (1 - core if other else core)

    partner, right, left = slot(0, True), slot(1), slot(-1)

    def other_samp(d):
        return lax.rem(samp + d, samps)

    def columns(j):
        return pl.ds(pl.multiple_of(j * block, block), block)

    def load_bases(j):
        at = bases.at[:, :, columns(j)]
        return pltpu.make_async_copy(bases_hbm.at[:, :, columns(j)], at, load_sem.at[j])

    loads = [
        pltpu.make_async_copy(mass_hbm, mass_row, load_sem.at[samps]),
        pltpu.make_async_copy(own_hbm, gathered.at[samp], load_sem.at[samps + 1]),
        pltpu.make_async_copy(weight_hbm, weight_ref, load_sem.at[samps + 2]),
    ]
    for load in loads:
        load.start()

    barrier = pltpu.get_barrier_semaphore()

    def along_x(d):
        return lax.rem(x + d, lines) * line + z

    def along_z(d):
        return x * line + lax.rem(z + d, line)

    for friend in (right, left, partner):
        pl.semaphore_signal(barrier, inc=1, device_id={"samp": friend}, device_id_type=MESH)
    for d in range(1, line):
        pl.semaphore_signal(barrier, inc=1, device_id={"cell": along_z(d)}, device_id_type=MESH)
    for d in range(1, lines):
        pl.semaphore_signal(barrier, inc=1, device_id={"cell": along_x(d)}, device_id_type=MESH)
    for friend in (slot(2), slot(1, True), slot(2, True), slot(-1, True)):
        pl.semaphore_signal(barrier, inc=1, device_id={"samp": friend}, device_id_type=MESH)

    for j in range(samps):
        load_bases(j).start()

    def weights(j):
        return mass_row[:, columns(j)] * (1.0 / depth)

    for load in loads:
        load.wait()
    mine = gathered.at[samp]
    pl.semaphore_wait(barrier, lines + line + samps - 3)

    def remote(src, dst, send_sem, recv_sem, **to):
        copy = pltpu.make_async_remote_copy(
            src_ref=src, dst_ref=dst, send_sem=send_sem, recv_sem=recv_sem, device_id=to, device_id_type=MESH
        )
        copy.start()
        return copy

    def send(src, dst, send_sem, recv_sem, to):
        return remote(src, dst, send_sem, recv_sem, samp=to)

    def arrived(ref, sem):
        pltpu.make_async_copy(ref, ref, sem).wait()

    def rows(h):
        return pl.ds(half * h, half)

    sent = []
    for h in (0, 1):
        sent.append(send(mine.at[rows(h)], mine.at[rows(h)], gather_send.at[h], gather_left.at[h], right))
        sent.append(send(mine.at[rows(1 - h)], mine.at[rows(1 - h)], gather_send.at[3 - h], gather_right.at[1 - h], left))
    sent.append(send(mine, mine, gather_send.at[4], gather_pair.at[0], partner))

    quarter = size // lines
    owners = quarter // 8

    class Reduction:
        def __init__(self, own, x_in, part, z_in, whole, sem, shift):
            self.own, self.x_in, self.part, self.z_in, self.whole = own, x_in, part, z_in, whole
            self.sent = [reduce_send.at[sem + i] for i in range(4)]
            self.recv = [reduce_recv.at[sem + i] for i in range(4)]
            self.shift = shift
            self.owns = self.is_owner(z)

        def is_owner(self, z_of):
            return (z_of >= self.shift) & (z_of < self.shift + owners)

        def rows(self, x_of, z_of=None):
            if z_of is None:
                return pl.ds(pl.multiple_of(quarter * x_of, 8), quarter)
            return pl.ds(pl.multiple_of(quarter * x_of + 8 * (z_of - self.shift), 8), 8)

        def small(self, z_of):
            return pl.ds(pl.multiple_of(8 * (z_of - self.shift), 8), 8)

        def count(self, n):
            return self.own.at[pl.ds(0, n)]

        def counted(self, owner, rest, sem):
            @pl.when(self.owns)
            def _():
                arrived(self.count(owner), sem)

            if rest:

                @pl.when(jnp.logical_not(self.owns))
                def _():
                    arrived(self.count(rest), sem)

        def scatter_x(self):
            for d in (2, 1, 3):
                to = lax.rem(x + d, lines)
                remote(self.own.at[self.rows(to)], self.x_in.at[x], self.sent[0], self.recv[0], cell=to * line + z)

        def scatter_z(self):
            self.x_in[x] = self.own[self.rows(x), :]
            arrived(self.count(quarter * (lines - 1)), self.recv[0])
            self.part[...] = jnp.sum(self.x_in[...], axis=0)
            for d in (4, 3, 5, 2, 6, 1, 7):
                to = lax.rem(z + d, line)

                @pl.when(self.is_owner(to))
                def _(to=to):
                    src = self.part.at[self.small(to)]
                    remote(src, self.z_in.at[z], self.sent[1], self.recv[1], cell=x * line + to)

        def total(self):
            self.z_in[z] = self.part[self.small(z), :]
            arrived(self.count(8 * (line - 1)), self.recv[1])
            return jnp.sum(self.z_in[...], axis=0)

        def share_z(self):
            piece = self.whole.at[self.rows(x, z)]
            for d in (4, 3, 5, 2, 6, 1, 7):
                remote(piece, piece, self.sent[2], self.recv[2], cell=along_z(d))

        def share_x(self):
            self.counted(quarter - 8, quarter, self.recv[2])
            piece = self.whole.at[self.rows(x)]
            for d in (2, 1, 3):
                remote(piece, piece, self.sent[3], self.recv[3], cell=along_x(d))

        def finish(self):
            arrived(self.count(quarter * (lines - 1)), self.recv[3])

        def drain(self):
            arrived(self.count(quarter * (lines - 1)), self.sent[0])
            self.counted(quarter - 8, quarter, self.sent[1])
            self.counted(8 * (line - 1), 0, self.sent[2])
            arrived(self.count(quarter * (lines - 1)), self.sent[3])

    sum_c = Reduction(gram, c_x, c_part, c_z, c_all, 0, 0)
    sum_g = Reduction(g_own, g_x, g_part, g_z, g_all, 4, line - owners)

    def spread_h():
        @pl.when(sum_g.owns)
        def _():
            total = sum_g.total()
            g_all[sum_g.rows(x, z), : 2 * size] = total[:, : 2 * size]
            h_in[samp] = total[:, 2 * size :]
            for d in range(1, samps):
                remote(h_in.at[samp], h_in.at[samp], reduce_send.at[8], reduce_recv.at[8], samp=other_samp(d))

    def share_g():
        @pl.when(sum_g.owns)
        def _():
            arrived(h_in.at[pl.ds(0, samps - 1)], reduce_recv.at[8])
            g_all[sum_g.rows(x, z), 2 * size :] = jnp.sum(h_in[...], axis=0)
            sum_g.share_z()

    def share_c():
        @pl.when(sum_c.owns)
        def _():
            c_all[sum_c.rows(x, z), :] = sum_c.total()
            sum_c.share_z()

    reference = mine[...]
    g_own[:, 2 * size :] = dot3(split(reference), split(reference * weights(samp)), NT)

    def own_gram(j, carry):
        load_bases(j).wait()
        mass = weights(j)
        for s in range(2):
            value = bases[s, :, columns(j)]
            high, low = split(value)
            at = pl.ds(size * (s + 1), size)
            zh[j, at, :] = high
            zl[j, at, :] = low
            curv[s] += dot3((high, low), split(value * mass), NT)
        return carry


    def cross(j, first=False):
        value = gathered[j]
        high, low = split(value)
        zh[j, pl.ds(0, size), :] = high
        zl[j, pl.ds(0, size), :] = low
        at = pl.ds(size, 2 * size)
        term = dot3(split(value * weights(j)), (zh[j, at, :], zl[j, at, :]), NT)
        if first:
            gram[...] = term
        else:
            gram[...] += term

    curv[...] = jnp.zeros_like(curv)
    lax.fori_loop(0, samps // 2, own_gram, 0)
    from_left, from_right, far = gathered.at[left], gathered.at[right], gathered.at[slot(2)]
    arrived(mine.at[rows(0)], gather_left.at[0])
    sent.append(send(from_left.at[rows(0)], from_left.at[rows(0)], gather_send.at[5], gather_far.at[0], right))
    arrived(mine.at[rows(1)], gather_right.at[1])
    sent.append(send(from_right.at[rows(1)], from_right.at[rows(1)], gather_send.at[6], gather_far.at[1], left))
    lax.fori_loop(samps // 2, samps, own_gram, 0)
    g_own[:, : 2 * size] = pack(curv[0], curv[1])
    sum_g.scatter_x()
    arrived(mine.at[rows(1)], gather_left.at[1])
    sent.append(send(from_left, from_left, gather_send.at[7], gather_pair.at[1], partner))
    arrived(mine.at[rows(0)], gather_right.at[0])
    sent.append(send(from_right, from_right, gather_send.at[8], gather_pair.at[2], partner))
    arrived(mine, gather_pair.at[0])
    cross(samp, True)
    cross(partner)
    cross(left)
    cross(right)
    arrived(mine.at[rows(0)], gather_far.at[0])
    arrived(mine.at[rows(1)], gather_far.at[1])
    sent.append(send(far, far, gather_send.at[9], gather_pair.at[3], partner))
    sum_g.scatter_z()
    cross(slot(2))
    for i, step in ((1, -1), (2, 1), (3, 2)):
        arrived(mine, gather_pair.at[i])
        cross(slot(step, True))

    sum_c.scatter_x()
    spread_h()
    sum_c.scatter_z()
    share_c()
    sum_c.share_x()
    share_g()
    sum_c.finish()

    cross_gram = [c_all[:, :size], c_all[:, size:]]
    normal = [exact(c, c, NT) for c in cross_gram]
    minus_inverse = invert(normal, leaf, sum_g.share_x)
    turned = [-exact(m, c) for m, c in zip(minus_inverse, cross_gram)]

    sum_g.finish()
    of_bases = unpack(g_all[:, : 2 * size])
    of_reference = g_all[:, 2 * size :]
    plain = jnp.zeros((size, size), F32)
    for s in range(2):
        pieces = split(turned[s])
        middle = dot3(split(of_bases[s]), pieces, NT)
        curvature = dot3(pieces, split(middle)) - 2.0 * dot3(pieces, split(cross_gram[s]), NT) + of_reference
        factors = series(curvature) * weight_ref[s]
        plain = plain - factors
        lhs_h[s + 1], lhs_l[s + 1] = split(dot3(split(factors), pieces))
    lhs_h[0], lhs_l[0] = split(plain)

    def term(j):
        total = None
        for k in range(3):
            at = pl.ds(size * k, size)
            part = dot3((lhs_h[k], lhs_l[k]), (zh[j, at, :], zl[j, at, :]))
            total = part if total is None else total + part
        return total

    steps = (2, 1, -1, 0)
    for i, step in enumerate(steps):
        pair_out[i] = term(slot(step, True))
        sent.append(send(pair_out.at[i], pair_in.at[i], final_send.at[i], final_pair.at[i], partner))

    def own_term(i):
        value = term(slot(steps[i]))
        arrived(pair_in.at[i], final_pair.at[i])
        return value + pair_in[i]

    def forward(i, h, to, sem, recv, dst):
        sent.append(send(sums.at[i, rows(h)], dst, final_send.at[sem], recv, to))

    sums[0] = own_term(0)
    forward(0, 0, right, 4, final_far.at[0], far_in.at[0])
    forward(0, 1, left, 5, final_far.at[1], far_in.at[1])
    sums[1] = own_term(1)
    forward(1, 1, right, 6, final_near.at[1], near_in.at[0, rows(1)])
    sums[2] = own_term(2)
    forward(2, 0, left, 7, final_near.at[2], near_in.at[1, rows(0)])
    arrived(far_in.at[0], final_far.at[0])
    sums[1, rows(0), :] += far_in[0]
    forward(1, 0, right, 8, final_near.at[0], near_in.at[0, rows(0)])
    arrived(far_in.at[1], final_far.at[1])
    sums[2, rows(1), :] += far_in[1]
    forward(2, 1, left, 9, final_near.at[3], near_in.at[1, rows(1)])
    out_ref[...] = own_term(3)
    for i in range(4):
        arrived(far_in.at[0], final_near.at[i])
    out_ref[...] += near_in[0] + near_in[1]

    for copy in sent:
        copy.wait_send()
    sum_c.drain()
    sum_g.drain()

    @pl.when(sum_g.owns)
    def _():
        arrived(h_in.at[pl.ds(0, samps - 1)], reduce_send.at[8])


def body(bases, reference_basis, mass, interp_weights):
    cells, samps = lax.axis_size("cell"), lax.axis_size("samp")
    count, depth, size = bases.shape
    block = reference_basis.shape[0]
    packed, wide = 2 * size, 3 * size
    half = size // 2
    hbm, vmem = pl.BlockSpec(memory_space=pltpu.HBM), pl.BlockSpec(memory_space=pltpu.VMEM)
    line = 8
    lines = cells // line
    result = pl.pallas_call(
        functools.partial(kernel, cells, depth * cells, samps),
        out_shape=jax.ShapeDtypeStruct((size, block), F32),
        in_specs=[hbm] * 4,
        out_specs=vmem,
        scratch_shapes=[
            pltpu.VMEM((count, size, depth), F32),
            pltpu.VMEM((1, depth), F32),
            pltpu.SMEM((count,), F32),
            pltpu.VMEM((samps, size, block), F32),
            pltpu.VMEM((samps, 3 * size, block), BF16),
            pltpu.VMEM((samps, 3 * size, block), BF16),
            pltpu.VMEM((size, packed), F32),
            pltpu.VMEM((2, size, size), F32),
            pltpu.VMEM((lines, size // lines, packed), F32),
            pltpu.VMEM((size // lines, packed), F32),
            pltpu.VMEM((line, 8, packed), F32),
            pltpu.VMEM((size, packed), F32),
            pltpu.VMEM((size, wide), F32),
            pltpu.VMEM((lines, size // lines, wide), F32),
            pltpu.VMEM((size // lines, wide), F32),
            pltpu.VMEM((line, 8, wide), F32),
            pltpu.VMEM((samps, 8, size), F32),
            pltpu.VMEM((size, wide), F32),
            pltpu.VMEM((LEAF, 2 * LEAF), F32),
            pltpu.VMEM((3, size, size), BF16),
            pltpu.VMEM((3, size, size), BF16),
            pltpu.VMEM((4, size, block), F32),
            pltpu.VMEM((4, size, block), F32),
            pltpu.VMEM((3, size, block), F32),
            pltpu.VMEM((2, half, block), F32),
            pltpu.VMEM((2, size, block), F32),
            pltpu.SemaphoreType.DMA((samps + 3,)),
            pltpu.SemaphoreType.DMA((10,)),
            pltpu.SemaphoreType.DMA((2,)),
            pltpu.SemaphoreType.DMA((2,)),
            pltpu.SemaphoreType.DMA((2,)),
            pltpu.SemaphoreType.DMA((4,)),
            pltpu.SemaphoreType.DMA((9,)),
            pltpu.SemaphoreType.DMA((9,)),
            pltpu.SemaphoreType.DMA((10,)),
            pltpu.SemaphoreType.DMA((4,)),
            pltpu.SemaphoreType.DMA((2,)),
            pltpu.SemaphoreType.DMA((4,)),
        ],
        compiler_params=pltpu.CompilerParams(
            collective_id=0, has_side_effects=True, vmem_limit_bytes=48 * 1024 * 1024
        ),
    )(jnp.swapaxes(bases, 1, 2), reference_basis.T, mass[None, :], interp_weights)
    return result.T


def solution(mesh):
    placed = (P("samp", "cell", None), P(("cell", "samp"), None), P("cell"), P("samp"))
    return jax.shard_map(
        body, mesh=mesh, in_specs=placed, out_specs=P(("cell", "samp"), None), check_vma=False
    )
```

```python
import functools

import jax
import jax.numpy as jnp
from jax import lax
from jax.experimental import pallas as pl
from jax.experimental.pallas import tpu as pltpu
from jax.sharding import PartitionSpec as P

NTERMS = 6
MESH = pl.DeviceIdType.MESH
F32, BF16 = jnp.float32, jnp.bfloat16
HIGHEST = lax.Precision.HIGHEST
NN = (((1,), (0,)), ((), ()))
NT = (((1,), (1,)), ((), ()))
LEAF = 64


def split(x):
    high = x.astype(BF16)
    return high, (x - high.astype(F32)).astype(BF16)


def dot(a, b, dims=NN):
    return lax.dot_general(a, b, dims, preferred_element_type=F32)


def dot3(a, b, dims=NN):
    (ah, al), (bh, bl) = a, b
    return dot(ah, bh, dims) + (dot(ah, bl, dims) + dot(al, bh, dims))


def matmul(a, b):
    return dot3(split(a), split(b))


def exact(a, b, dims=NN):
    return lax.dot_general(a, b, dims, precision=HIGHEST, preferred_element_type=F32)


def pack(first, second):
    middle = jnp.concatenate([first[:, 128:], second[:, 128:]], axis=1)
    return jnp.concatenate([first[:, :128], middle, second[:, :128]], axis=1)


def unpack(packed):
    middle = packed[:, 128:256]
    half = middle.shape[1] // 2
    first = jnp.concatenate([packed[:, :128], middle[:, :half]], axis=1)
    second = jnp.concatenate([packed[:, 256:384], middle[:, half:]], axis=1)
    return first, second


def sweep_leaf(leaf_ref):
    lane = lax.broadcasted_iota(jnp.int32, (8, 128), 1)
    row = lax.broadcasted_iota(jnp.int32, (8, 128), 0)
    within = lane & (LEAF - 1)
    start = lane - within

    def step(p, carry):
        first = 8 * p
        index = [start + first + c for c in range(8)]
        own = pl.ds(pl.multiple_of(first, 8), 8)
        pivot = leaf_ref[own, :]

        def column(x, c):
            return jnp.take_along_axis(x, index[c], axis=1, mode="promise_in_bounds")

        columns = [column(pivot, c) for c in range(8)]
        e = {
            (r, c): jnp.broadcast_to(columns[c][r : r + 1, :], (8, 128))
            for c in range(8)
            for r in range(c + 1)
        }

        def at(r, c):
            return (r, c) if r <= c else (c, r)

        for k in range(8):
            inverse = 1.0 / e[k, k]
            scaled = {j: e[at(k, j)] * inverse for j in range(8) if j != k}
            for j in range(8):
                for i in range(j + 1):
                    if i != k and j != k:
                        e[i, j] = e[i, j] - e[at(i, k)] * scaled[j]
            for j in scaled:
                e[at(k, j)] = scaled[j]
            e[k, k] = -inverse

        inside = (within >= first) & (within < first + 8)
        rows = [
            jnp.where(
                within == first + c,
                1.0,
                jnp.where(inside, 0.0, -jnp.broadcast_to(pivot[c : c + 1, :], (8, 128))),
            )
            for c in range(8)
        ]
        scaled_rows = []
        for r in range(8):
            total = e[at(r, 0)] * rows[0]
            for c in range(1, 8):
                total = total + e[at(r, c)] * rows[c]
            scaled_rows.append(total)
        for g in range(LEAF // 8):
            block = leaf_ref[8 * g : 8 * g + 8, :]
            total = jnp.where(inside, 0.0, block)
            for c in range(8):
                total = total - column(block, c) * scaled_rows[c]
            leaf_ref[8 * g : 8 * g + 8, :] = total
        joined = scaled_rows[0]
        for r in range(1, 8):
            joined = jnp.where(row == r, scaled_rows[r], joined)
        leaf_ref[own, :] = joined
        return carry

    lax.fori_loop(0, LEAF // 8, step, 0)


def invert(normal, leaf_ref, between):
    size = normal[0].shape[0]
    row = lax.broadcasted_iota(jnp.int32, (LEAF, size), 0)
    lane = lax.broadcasted_iota(jnp.int32, (LEAF, size), 1)
    every_lane = lax.broadcasted_iota(jnp.int32, (size, size), 1)
    for i in range(size // LEAF):
        own = slice(LEAF * i, LEAF * (i + 1))
        leaf_ref[...] = jnp.concatenate([n[own, own] for n in normal], axis=1)
        sweep_leaf(leaf_ref)
        if i == 0:
            between()
        minus_inverse = leaf_ref[...]
        inside = (lane >= LEAF * i) & (lane < LEAF * (i + 1))
        panels = [jnp.where(lane == row + LEAF * i, 1.0, jnp.where(inside, 0.0, -n[own, :])) for n in normal]
        scaled = [exact(minus_inverse[:, LEAF * s : LEAF * (s + 1)], panels[s]) for s in range(2)]
        cleared = (every_lane >= LEAF * i) & (every_lane < LEAF * (i + 1))
        products = [exact(n[:, own], r) for n, r in zip(normal, scaled)]
        updated = []
        for n, r, product in zip(normal, scaled, products):
            new = jnp.where(cleared, 0.0, n) - product
            parts = [new[: LEAF * i], r, new[LEAF * (i + 1) :]]
            updated.append(jnp.concatenate([part for part in parts if part.shape[0]], axis=0))
        normal = updated
    return normal


def series(curvatures):
    size = curvatures[0].shape[0]
    diagonal = lax.broadcasted_iota(jnp.int32, (size, size), 0) == lax.broadcasted_iota(jnp.int32, (size, size), 1)
    weight = [(-1.0) ** n / (2 * n + 1) for n in range(NTERMS)]

    def pair(curvature, n):
        return weight[n + 1] * curvature + jnp.where(diagonal, weight[n], 0.0)

    pieces = [split(c) for c in curvatures]
    squares = [split(dot3(p, p)) for p in pieces]
    results = [pair(c, NTERMS - 2) for c in curvatures]
    for n in range(NTERMS - 4, -1, -2):
        products = [dot3(square, split(r)) for square, r in zip(squares, results)]
        results = [pair(c, n) + product for c, product in zip(curvatures, products)]
    return results


def kernel(
    cells,
    depth,
    samps,
    bases_hbm,
    own_hbm,
    mass_hbm,
    weight_hbm,
    out_ref,
    bases,
    mass_row,
    weight_ref,
    gathered,
    zh,
    zl,
    gram,
    curv,
    c_x,
    c_part,
    c_z,
    c_all,
    g_own,
    g_x,
    g_part,
    g_z,
    h_pair,
    h_in,
    g_all,
    leaf,
    lhs_h,
    lhs_l,
    pair_out,
    pair_in,
    sums,
    far_in,
    near_in,
    load_sem,
    gather_send,
    gather_left,
    gather_right,
    gather_far,
    gather_pair,
    reduce_send,
    reduce_recv,
    final_send,
    final_pair,
    final_far,
    final_near,
):
    size, block = own_hbm.shape
    half = size // 2
    cell = lax.axis_index("cell")
    samp = lax.axis_index("samp")
    chips = samps // 2
    core = lax.rem(samp, 2)
    y = samp // 2
    line = 8
    lines = cells // line
    x, z = cell // line, lax.rem(cell, line)

    def there(step):
        return lax.rem(y + step + chips, chips)

    def slot(step, other=False):
        return 2 * there(step) + (1 - core if other else core)

    partner, right, left = slot(0, True), slot(1), slot(-1)

    def columns(j):
        return pl.ds(pl.multiple_of(j * block, block), block)

    def load_bases(h):
        at = pl.ds(h * block * (samps // 2), block * (samps // 2))
        return pltpu.make_async_copy(bases_hbm.at[:, :, at], bases.at[:, :, at], load_sem.at[h])

    loads = [
        pltpu.make_async_copy(mass_hbm, mass_row, load_sem.at[2]),
        pltpu.make_async_copy(own_hbm, gathered.at[samp], load_sem.at[3]),
        pltpu.make_async_copy(weight_hbm, weight_ref, load_sem.at[4]),
    ]
    for load in loads:
        load.start()

    barrier = pltpu.get_barrier_semaphore()

    def along_x(d):
        return lax.rem(x + d, lines) * line + z

    def along_z(d):
        return x * line + lax.rem(z + d, line)

    for friend in (right, left, partner, slot(2)):
        pl.semaphore_signal(barrier, inc=1, device_id={"samp": friend}, device_id_type=MESH)
    for d in range(1, line):
        pl.semaphore_signal(barrier, inc=1, device_id={"cell": along_z(d)}, device_id_type=MESH)
    for d in range(1, lines):
        pl.semaphore_signal(barrier, inc=1, device_id={"cell": along_x(d)}, device_id_type=MESH)

    def weights(j):
        return mass_row[:, columns(j)] * (1.0 / depth)

    for load in loads:
        load.wait()
    mine = gathered.at[samp]
    pl.semaphore_wait(barrier, lines + line + chips - 2)

    def remote(src, dst, send_sem, recv_sem, **to):
        copy = pltpu.make_async_remote_copy(
            src_ref=src, dst_ref=dst, send_sem=send_sem, recv_sem=recv_sem, device_id=to, device_id_type=MESH
        )
        copy.start()
        return copy

    def send(src, dst, send_sem, recv_sem, to):
        return remote(src, dst, send_sem, recv_sem, samp=to)

    def arrived(ref, sem):
        pltpu.make_async_copy(ref, ref, sem).wait()

    def rows(h):
        return pl.ds(half * h, half)

    sent = []
    for h in (0, 1):
        sent.append(send(mine.at[rows(h)], mine.at[rows(h)], gather_send.at[h], gather_left.at[h], right))
        sent.append(send(mine.at[rows(1 - h)], mine.at[rows(1 - h)], gather_send.at[3 - h], gather_right.at[1 - h], left))
    sent.append(send(mine, mine, gather_send.at[4], gather_pair.at[0], partner))

    for h in (0, 1):
        load_bases(h).start()

    quarter = size // lines
    owners = quarter // 8

    class Reduction:
        def __init__(self, own, x_in, part, z_in, whole, sem, shift):
            self.own, self.x_in, self.part, self.z_in, self.whole = own, x_in, part, z_in, whole
            self.sent = [reduce_send.at[sem + i] for i in range(4)]
            self.recv = [reduce_recv.at[sem + i] for i in range(4)]
            self.shift = shift
            self.owns = self.is_owner(z)

        def is_owner(self, z_of):
            return (z_of >= self.shift) & (z_of < self.shift + owners)

        def rows(self, x_of, z_of=None):
            if z_of is None:
                return pl.ds(pl.multiple_of(quarter * x_of, 8), quarter)
            return pl.ds(pl.multiple_of(quarter * x_of + 8 * (z_of - self.shift), 8), 8)

        def small(self, z_of):
            return pl.ds(pl.multiple_of(8 * (z_of - self.shift), 8), 8)

        def count(self, n):
            return self.own.at[pl.ds(0, n)]

        def counted(self, owner, rest, sem):
            @pl.when(self.owns)
            def _():
                arrived(self.count(owner), sem)

            if rest:

                @pl.when(jnp.logical_not(self.owns))
                def _():
                    arrived(self.count(rest), sem)

        def scatter_x(self):
            for d in (2, 1, 3):
                to = lax.rem(x + d, lines)
                remote(self.own.at[self.rows(to)], self.x_in.at[x], self.sent[0], self.recv[0], cell=to * line + z)

        def scatter_z(self):
            self.x_in[x] = self.own[self.rows(x), :]
            arrived(self.count(quarter * (lines - 1)), self.recv[0])
            self.part[...] = jnp.sum(self.x_in[...], axis=0)
            for d in (4, 3, 5, 2, 6, 1, 7):
                to = lax.rem(z + d, line)

                @pl.when(self.is_owner(to))
                def _(to=to):
                    src = self.part.at[self.small(to)]
                    remote(src, self.z_in.at[z], self.sent[1], self.recv[1], cell=x * line + to)

        def total(self):
            self.z_in[z] = self.part[self.small(z), :]
            arrived(self.count(8 * (line - 1)), self.recv[1])
            return jnp.sum(self.z_in[...], axis=0)

        def share_z(self):
            piece = self.whole.at[self.rows(x, z)]
            for d in (4, 3, 5, 2, 6, 1, 7):
                remote(piece, piece, self.sent[2], self.recv[2], cell=along_z(d))

        def share_x(self):
            self.counted(quarter - 8, quarter, self.recv[2])
            piece = self.whole.at[self.rows(x)]
            for d in (2, 1, 3):
                remote(piece, piece, self.sent[3], self.recv[3], cell=along_x(d))

        def finish(self):
            arrived(self.count(quarter * (lines - 1)), self.recv[3])

        def drain(self):
            arrived(self.count(quarter * (lines - 1)), self.sent[0])
            self.counted(quarter - 8, quarter, self.sent[1])
            self.counted(8 * (line - 1), 0, self.sent[2])
            arrived(self.count(quarter * (lines - 1)), self.sent[3])

    sum_c = Reduction(gram, c_x, c_part, c_z, c_all, 0, 0)
    sum_g = Reduction(g_own, g_x, g_part, g_z, g_all, 4, line - owners)

    def spread_h():
        @pl.when(sum_g.owns)
        def _():
            total = sum_g.total()
            g_all[sum_g.rows(x, z), : 2 * size] = total[:, : 2 * size]
            h_pair[0] = total[:, 2 * size :]
            remote(h_pair.at[0], h_pair.at[1], reduce_send.at[8], reduce_recv.at[8], samp=partner)

    def spread_pair():
        @pl.when(sum_g.owns)
        def _():
            arrived(h_pair.at[0], reduce_recv.at[8])
            h_in[y] = h_pair[0] + h_pair[1]
            for step in (2, 1, -1):
                remote(h_in.at[y], h_in.at[y], reduce_send.at[9], reduce_recv.at[9], samp=slot(step))

    def share_g():
        @pl.when(sum_g.owns)
        def _():
            arrived(h_in.at[pl.ds(0, chips - 1)], reduce_recv.at[9])
            g_all[sum_g.rows(x, z), 2 * size :] = jnp.sum(h_in[...], axis=0)
            sum_g.share_z()

    def share_c():
        @pl.when(sum_c.owns)
        def _():
            c_all[sum_c.rows(x, z), :] = sum_c.total()
            sum_c.share_z()

    reference = mine[...]
    g_own[:, 2 * size :] = dot3(split(reference), split(reference * weights(samp)), NT)

    def own_gram(j, carry):
        mass = weights(j)
        for s in range(2):
            value = bases[s, :, columns(j)]
            high, low = split(value)
            at = pl.ds(size * (s + 1), size)
            zh[j, at, :] = high
            zl[j, at, :] = low
            curv[s] += dot3((high, low), split(value * mass), NT)
        return carry


    def cross(j, first=False):
        value = gathered[j]
        high, low = split(value)
        zh[j, pl.ds(0, size), :] = high
        zl[j, pl.ds(0, size), :] = low
        at = pl.ds(size, 2 * size)
        term = dot3(split(value * weights(j)), (zh[j, at, :], zl[j, at, :]), NT)
        if first:
            gram[...] = term
        else:
            gram[...] += term

    curv[...] = jnp.zeros_like(curv)
    load_bases(0).wait()
    lax.fori_loop(0, samps // 2, own_gram, 0)
    from_left, from_right, far = gathered.at[left], gathered.at[right], gathered.at[slot(2)]
    arrived(mine.at[rows(0)], gather_left.at[0])
    sent.append(send(from_left.at[rows(0)], from_left.at[rows(0)], gather_send.at[5], gather_far.at[0], right))
    arrived(mine.at[rows(1)], gather_right.at[1])
    sent.append(send(from_right.at[rows(1)], from_right.at[rows(1)], gather_send.at[6], gather_far.at[1], left))
    load_bases(1).wait()
    lax.fori_loop(samps // 2, samps, own_gram, 0)
    g_own[:, : 2 * size] = pack(curv[0], curv[1])
    sum_g.scatter_x()
    arrived(mine.at[rows(1)], gather_left.at[1])
    sent.append(send(from_left, from_left, gather_send.at[7], gather_pair.at[1], partner))
    arrived(mine.at[rows(0)], gather_right.at[0])
    sent.append(send(from_right, from_right, gather_send.at[8], gather_pair.at[2], partner))
    arrived(mine, gather_pair.at[0])
    cross(samp, True)
    cross(partner)
    cross(left)
    cross(right)
    arrived(mine.at[rows(0)], gather_far.at[0])
    arrived(mine.at[rows(1)], gather_far.at[1])
    sent.append(send(far, far, gather_send.at[9], gather_pair.at[3], partner))
    sum_g.scatter_z()
    cross(slot(2))
    for i, step in ((1, -1), (2, 1), (3, 2)):
        arrived(mine, gather_pair.at[i])
        cross(slot(step, True))

    sum_c.scatter_x()
    spread_h()
    sum_c.scatter_z()
    spread_pair()
    share_c()
    sum_c.share_x()
    share_g()
    sum_c.finish()
    sum_g.share_x()

    cross_gram = [c_all[:, :size], c_all[:, size:]]
    normal = [exact(c, c, NT) for c in cross_gram]
    minus_inverse = invert(normal, leaf, lambda: None)
    turned = [-exact(m, c) for m, c in zip(minus_inverse, cross_gram)]

    sum_g.finish()
    of_bases = unpack(g_all[:, : 2 * size])
    of_reference = g_all[:, 2 * size :]
    pieces = [split(t) for t in turned]
    middles = [dot3(split(g), p, NT) for g, p in zip(of_bases, pieces)]
    mixed = [dot3(p, split(c), NT) for p, c in zip(pieces, cross_gram)]
    outer = [dot3(p, split(m)) for p, m in zip(pieces, middles)]
    results = series([o - 2.0 * m + of_reference for o, m in zip(outer, mixed)])
    factors = [f * weight_ref[s] for s, f in enumerate(results)]
    plain = -(factors[0] + factors[1])
    finals = [dot3(split(f), p) for f, p in zip(factors, pieces)]
    for s in range(2):
        lhs_h[s + 1], lhs_l[s + 1] = split(finals[s])
    lhs_h[0], lhs_l[0] = split(plain)

    def term(j):
        total = None
        for k in range(3):
            at = pl.ds(size * k, size)
            part = dot3((lhs_h[k], lhs_l[k]), (zh[j, at, :], zl[j, at, :]))
            total = part if total is None else total + part
        return total

    steps = (2, 1, -1, 0)
    for i, step in enumerate(steps):
        pair_out[i] = term(slot(step, True))
        sent.append(send(pair_out.at[i], pair_in.at[i], final_send.at[i], final_pair.at[i], partner))

    def own_term(i):
        value = term(slot(steps[i]))
        arrived(pair_in.at[i], final_pair.at[i])
        return value + pair_in[i]

    def forward(i, h, to, sem, recv, dst):
        sent.append(send(sums.at[i, rows(h)], dst, final_send.at[sem], recv, to))

    sums[0] = own_term(0)
    forward(0, 0, right, 4, final_far.at[0], far_in.at[0])
    forward(0, 1, left, 5, final_far.at[1], far_in.at[1])
    sums[1] = own_term(1)
    forward(1, 1, right, 6, final_near.at[1], near_in.at[0, rows(1)])
    sums[2] = own_term(2)
    forward(2, 0, left, 7, final_near.at[2], near_in.at[1, rows(0)])
    arrived(far_in.at[0], final_far.at[0])
    sums[1, rows(0), :] += far_in[0]
    forward(1, 0, right, 8, final_near.at[0], near_in.at[0, rows(0)])
    arrived(far_in.at[1], final_far.at[1])
    sums[2, rows(1), :] += far_in[1]
    forward(2, 1, left, 9, final_near.at[3], near_in.at[1, rows(1)])
    out_ref[...] = own_term(3)
    for i in range(4):
        arrived(far_in.at[0], final_near.at[i])
    out_ref[...] += near_in[0] + near_in[1]

    for copy in sent:
        copy.wait_send()
    sum_c.drain()
    sum_g.drain()

    @pl.when(sum_g.owns)
    def _():
        arrived(h_pair.at[0], reduce_send.at[8])
        arrived(h_in.at[pl.ds(0, chips - 1)], reduce_send.at[9])


def body(bases, reference_basis, mass, interp_weights):
    cells, samps = lax.axis_size("cell"), lax.axis_size("samp")
    count, depth, size = bases.shape
    block = reference_basis.shape[0]
    packed, wide = 2 * size, 3 * size
    half = size // 2
    hbm, vmem = pl.BlockSpec(memory_space=pltpu.HBM), pl.BlockSpec(memory_space=pltpu.VMEM)
    line = 8
    lines = cells // line
    result = pl.pallas_call(
        functools.partial(kernel, cells, depth * cells, samps),
        out_shape=jax.ShapeDtypeStruct((size, block), F32),
        in_specs=[hbm] * 4,
        out_specs=vmem,
        scratch_shapes=[
            pltpu.VMEM((count, size, depth), F32),
            pltpu.VMEM((1, depth), F32),
            pltpu.SMEM((count,), F32),
            pltpu.VMEM((samps, size, block), F32),
            pltpu.VMEM((samps, 3 * size, block), BF16),
            pltpu.VMEM((samps, 3 * size, block), BF16),
            pltpu.VMEM((size, packed), F32),
            pltpu.VMEM((2, size, size), F32),
            pltpu.VMEM((lines, size // lines, packed), F32),
            pltpu.VMEM((size // lines, packed), F32),
            pltpu.VMEM((line, 8, packed), F32),
            pltpu.VMEM((size, packed), F32),
            pltpu.VMEM((size, wide), F32),
            pltpu.VMEM((lines, size // lines, wide), F32),
            pltpu.VMEM((size // lines, wide), F32),
            pltpu.VMEM((line, 8, wide), F32),
            pltpu.VMEM((2, 8, size), F32),
            pltpu.VMEM((samps // 2, 8, size), F32),
            pltpu.VMEM((size, wide), F32),
            pltpu.VMEM((LEAF, 2 * LEAF), F32),
            pltpu.VMEM((3, size, size), BF16),
            pltpu.VMEM((3, size, size), BF16),
            pltpu.VMEM((4, size, block), F32),
            pltpu.VMEM((4, size, block), F32),
            pltpu.VMEM((3, size, block), F32),
            pltpu.VMEM((2, half, block), F32),
            pltpu.VMEM((2, size, block), F32),
            pltpu.SemaphoreType.DMA((5,)),
            pltpu.SemaphoreType.DMA((10,)),
            pltpu.SemaphoreType.DMA((2,)),
            pltpu.SemaphoreType.DMA((2,)),
            pltpu.SemaphoreType.DMA((2,)),
            pltpu.SemaphoreType.DMA((4,)),
            pltpu.SemaphoreType.DMA((10,)),
            pltpu.SemaphoreType.DMA((10,)),
            pltpu.SemaphoreType.DMA((10,)),
            pltpu.SemaphoreType.DMA((4,)),
            pltpu.SemaphoreType.DMA((2,)),
            pltpu.SemaphoreType.DMA((4,)),
        ],
        compiler_params=pltpu.CompilerParams(
            collective_id=0, has_side_effects=True, vmem_limit_bytes=48 * 1024 * 1024
        ),
    )(jnp.swapaxes(bases, 1, 2), reference_basis.T, mass[None, :], interp_weights)
    return result.T


def solution(mesh):
    placed = (P("samp", "cell", None), P(("cell", "samp"), None), P("cell"), P("samp"))
    return jax.shard_map(
        body, mesh=mesh, in_specs=placed, out_specs=P(("cell", "samp"), None), check_vma=False
    )
```

```python
import functools

import jax
import jax.numpy as jnp
from jax import lax
from jax.experimental import pallas as pl
from jax.experimental.pallas import tpu as pltpu
from jax.sharding import PartitionSpec as P

NTERMS = 6
MESH = pl.DeviceIdType.MESH
F32, BF16 = jnp.float32, jnp.bfloat16
HIGHEST = lax.Precision.HIGHEST
NN = (((1,), (0,)), ((), ()))
NT = (((1,), (1,)), ((), ()))
LEAF = 64


def split(x):
    high = x.astype(BF16)
    return high, (x - high.astype(F32)).astype(BF16)


def dot(a, b, dims=NN):
    return lax.dot_general(a, b, dims, preferred_element_type=F32)


def dot3(a, b, dims=NN):
    (ah, al), (bh, bl) = a, b
    return dot(ah, bh, dims) + (dot(ah, bl, dims) + dot(al, bh, dims))


def matmul(a, b):
    return dot3(split(a), split(b))


def exact(a, b, dims=NN):
    return lax.dot_general(a, b, dims, precision=HIGHEST, preferred_element_type=F32)


def pack(first, second):
    middle = jnp.concatenate([first[:, 128:], second[:, 128:]], axis=1)
    return jnp.concatenate([first[:, :128], middle, second[:, :128]], axis=1)


def unpack(packed):
    middle = packed[:, 128:256]
    half = middle.shape[1] // 2
    first = jnp.concatenate([packed[:, :128], middle[:, :half]], axis=1)
    second = jnp.concatenate([packed[:, 256:384], middle[:, half:]], axis=1)
    return first, second


def sweep_leaf(leaf_ref):
    lane = lax.broadcasted_iota(jnp.int32, (8, 128), 1)
    row = lax.broadcasted_iota(jnp.int32, (8, 128), 0)
    within = lane & (LEAF - 1)
    start = lane - within

    def step(p, carry):
        first = 8 * p
        index = [start + first + c for c in range(8)]
        own = pl.ds(pl.multiple_of(first, 8), 8)
        pivot = leaf_ref[own, :]

        def column(x, c):
            return jnp.take_along_axis(x, index[c], axis=1, mode="promise_in_bounds")

        columns = [column(pivot, c) for c in range(8)]
        e = {
            (r, c): jnp.broadcast_to(columns[c][r : r + 1, :], (8, 128))
            for c in range(8)
            for r in range(c + 1)
        }

        def at(r, c):
            return (r, c) if r <= c else (c, r)

        for k in range(8):
            inverse = 1.0 / e[k, k]
            scaled = {j: e[at(k, j)] * inverse for j in range(8) if j != k}
            for j in range(8):
                for i in range(j + 1):
                    if i != k and j != k:
                        e[i, j] = e[i, j] - e[at(i, k)] * scaled[j]
            for j in scaled:
                e[at(k, j)] = scaled[j]
            e[k, k] = -inverse

        inside = (within >= first) & (within < first + 8)
        rows = [
            jnp.where(
                within == first + c,
                1.0,
                jnp.where(inside, 0.0, -jnp.broadcast_to(pivot[c : c + 1, :], (8, 128))),
            )
            for c in range(8)
        ]
        scaled_rows = []
        for r in range(8):
            total = e[at(r, 0)] * rows[0]
            for c in range(1, 8):
                total = total + e[at(r, c)] * rows[c]
            scaled_rows.append(total)
        for g in range(LEAF // 8):
            block = leaf_ref[8 * g : 8 * g + 8, :]
            total = jnp.where(inside, 0.0, block)
            for c in range(8):
                total = total - column(block, c) * scaled_rows[c]
            leaf_ref[8 * g : 8 * g + 8, :] = total
        joined = scaled_rows[0]
        for r in range(1, 8):
            joined = jnp.where(row == r, scaled_rows[r], joined)
        leaf_ref[own, :] = joined
        return carry

    lax.fori_loop(0, LEAF // 8, step, 0)


def invert(normal, leaf_ref, between):
    size = normal[0].shape[0]
    row = lax.broadcasted_iota(jnp.int32, (LEAF, size), 0)
    lane = lax.broadcasted_iota(jnp.int32, (LEAF, size), 1)
    every_lane = lax.broadcasted_iota(jnp.int32, (size, size), 1)
    for i in range(size // LEAF):
        own = slice(LEAF * i, LEAF * (i + 1))
        leaf_ref[...] = jnp.concatenate([n[own, own] for n in normal], axis=1)
        sweep_leaf(leaf_ref)
        if i == 0:
            between()
        minus_inverse = leaf_ref[...]
        inside = (lane >= LEAF * i) & (lane < LEAF * (i + 1))
        panels = [jnp.where(lane == row + LEAF * i, 1.0, jnp.where(inside, 0.0, -n[own, :])) for n in normal]
        scaled = [exact(minus_inverse[:, LEAF * s : LEAF * (s + 1)], panels[s]) for s in range(2)]
        cleared = (every_lane >= LEAF * i) & (every_lane < LEAF * (i + 1))
        products = [exact(n[:, own], r) for n, r in zip(normal, scaled)]
        updated = []
        for n, r, product in zip(normal, scaled, products):
            new = jnp.where(cleared, 0.0, n) - product
            parts = [new[: LEAF * i], r, new[LEAF * (i + 1) :]]
            updated.append(jnp.concatenate([part for part in parts if part.shape[0]], axis=0))
        normal = updated
    return normal


def series(curvatures):
    size = curvatures[0].shape[0]
    diagonal = lax.broadcasted_iota(jnp.int32, (size, size), 0) == lax.broadcasted_iota(jnp.int32, (size, size), 1)
    weight = [(-1.0) ** n / (2 * n + 1) for n in range(NTERMS)]

    def pair(curvature, n):
        return weight[n + 1] * curvature + jnp.where(diagonal, weight[n], 0.0)

    pieces = [split(c) for c in curvatures]
    squares = [split(dot3(p, p)) for p in pieces]
    results = [pair(c, NTERMS - 2) for c in curvatures]
    for n in range(NTERMS - 4, -1, -2):
        products = [dot3(square, split(r)) for square, r in zip(squares, results)]
        results = [pair(c, n) + product for c, product in zip(curvatures, products)]
    return results


def kernel(
    cells,
    depth,
    samps,
    bases_hbm,
    own_hbm,
    mass_hbm,
    weight_hbm,
    out_ref,
    bases,
    mass_row,
    weight_ref,
    gathered,
    zh,
    zl,
    gram,
    curv,
    c_x,
    c_part,
    c_z,
    c_all,
    g_own,
    g_x,
    g_part,
    g_z,
    h_pair,
    h_in,
    g_all,
    leaf,
    lhs_h,
    lhs_l,
    pair_out,
    pair_in,
    sums,
    far_in,
    near_in,
    load_sem,
    gather_send,
    gather_left,
    gather_right,
    gather_far,
    gather_pair,
    reduce_send,
    reduce_recv,
    final_send,
    final_pair,
    final_far,
    final_near,
):
    size, block = own_hbm.shape
    half = size // 2
    cell = lax.axis_index("cell")
    samp = lax.axis_index("samp")
    chips = samps // 2
    core = lax.rem(samp, 2)
    y = samp // 2
    line = 8
    lines = cells // line
    x, z = cell // line, lax.rem(cell, line)

    def there(step):
        return lax.rem(y + step + chips, chips)

    def slot(step, other=False):
        return 2 * there(step) + (1 - core if other else core)

    partner, right, left = slot(0, True), slot(1), slot(-1)

    def columns(j):
        return pl.ds(pl.multiple_of(j * block, block), block)

    def load_bases(h):
        at = pl.ds(h * block * (samps // 2), block * (samps // 2))
        return pltpu.make_async_copy(bases_hbm.at[:, :, at], bases.at[:, :, at], load_sem.at[h])

    loads = [
        pltpu.make_async_copy(mass_hbm, mass_row, load_sem.at[2]),
        pltpu.make_async_copy(own_hbm, gathered.at[samp], load_sem.at[3]),
        pltpu.make_async_copy(weight_hbm, weight_ref, load_sem.at[4]),
    ]
    for load in loads:
        load.start()

    barrier = pltpu.get_barrier_semaphore()

    def along_x(d):
        return lax.rem(x + d, lines) * line + z

    def along_z(d):
        return x * line + lax.rem(z + d, line)

    for friend in (right, left, partner, slot(2)):
        pl.semaphore_signal(barrier, inc=1, device_id={"samp": friend}, device_id_type=MESH)
    for d in range(1, line):
        pl.semaphore_signal(barrier, inc=1, device_id={"cell": along_z(d)}, device_id_type=MESH)
    for d in range(1, lines):
        pl.semaphore_signal(barrier, inc=1, device_id={"cell": along_x(d)}, device_id_type=MESH)

    def weights(j):
        return mass_row[:, columns(j)] * (1.0 / depth)

    for load in loads:
        load.wait()
    mine = gathered.at[samp]
    pl.semaphore_wait(barrier, lines + line + chips - 2)

    def remote(src, dst, send_sem, recv_sem, **to):
        copy = pltpu.make_async_remote_copy(
            src_ref=src, dst_ref=dst, send_sem=send_sem, recv_sem=recv_sem, device_id=to, device_id_type=MESH
        )
        copy.start()
        return copy

    def send(src, dst, send_sem, recv_sem, to):
        return remote(src, dst, send_sem, recv_sem, samp=to)

    def arrived(ref, sem):
        pltpu.make_async_copy(ref, ref, sem).wait()

    def rows(h):
        return pl.ds(half * h, half)

    sent = []
    for h in (0, 1):
        sent.append(send(mine.at[rows(h)], mine.at[rows(h)], gather_send.at[h], gather_left.at[h], right))
        sent.append(send(mine.at[rows(1 - h)], mine.at[rows(1 - h)], gather_send.at[3 - h], gather_right.at[1 - h], left))
    sent.append(send(mine, mine, gather_send.at[4], gather_pair.at[0], partner))

    for h in (0, 1):
        load_bases(h).start()

    quarter = size // lines
    owners = quarter // 8

    class Reduction:
        def __init__(self, own, x_in, part, z_in, whole, sem, shift):
            self.own, self.x_in, self.part, self.z_in, self.whole = own, x_in, part, z_in, whole
            self.sent = [reduce_send.at[sem + i] for i in range(4)]
            self.recv = [reduce_recv.at[sem + i] for i in range(4)]
            self.shift = shift
            self.owns = self.is_owner(z)

        def is_owner(self, z_of):
            return (z_of >= self.shift) & (z_of < self.shift + owners)

        def rows(self, x_of, z_of=None):
            if z_of is None:
                return pl.ds(pl.multiple_of(quarter * x_of, 8), quarter)
            return pl.ds(pl.multiple_of(quarter * x_of + 8 * (z_of - self.shift), 8), 8)

        def small(self, z_of):
            return pl.ds(pl.multiple_of(8 * (z_of - self.shift), 8), 8)

        def count(self, n):
            return self.own.at[pl.ds(0, n)]

        def counted(self, owner, rest, sem):
            @pl.when(self.owns)
            def _():
                arrived(self.count(owner), sem)

            if rest:

                @pl.when(jnp.logical_not(self.owns))
                def _():
                    arrived(self.count(rest), sem)

        def scatter_x(self):
            for d in (2, 1, 3):
                to = lax.rem(x + d, lines)
                remote(self.own.at[self.rows(to)], self.x_in.at[x], self.sent[0], self.recv[0], cell=to * line + z)

        def scatter_z(self):
            self.x_in[x] = self.own[self.rows(x), :]
            arrived(self.count(quarter * (lines - 1)), self.recv[0])
            self.part[...] = jnp.sum(self.x_in[...], axis=0)
            for d in (4, 3, 5, 2, 6, 1, 7):
                to = lax.rem(z + d, line)

                @pl.when(self.is_owner(to))
                def _(to=to):
                    src = self.part.at[self.small(to)]
                    remote(src, self.z_in.at[z], self.sent[1], self.recv[1], cell=x * line + to)

        def total(self):
            self.z_in[z] = self.part[self.small(z), :]
            arrived(self.count(8 * (line - 1)), self.recv[1])
            return jnp.sum(self.z_in[...], axis=0)

        def share_z(self):
            piece = self.whole.at[self.rows(x, z)]
            for d in (4, 3, 5, 2, 6, 1, 7):
                remote(piece, piece, self.sent[2], self.recv[2], cell=along_z(d))

        def share_x(self):
            self.counted(quarter - 8, quarter, self.recv[2])
            piece = self.whole.at[self.rows(x)]
            for d in (2, 1, 3):
                remote(piece, piece, self.sent[3], self.recv[3], cell=along_x(d))

        def finish(self):
            arrived(self.count(quarter * (lines - 1)), self.recv[3])

        def drain(self):
            arrived(self.count(quarter * (lines - 1)), self.sent[0])
            self.counted(quarter - 8, quarter, self.sent[1])
            self.counted(8 * (line - 1), 0, self.sent[2])
            arrived(self.count(quarter * (lines - 1)), self.sent[3])

    sum_c = Reduction(gram, c_x, c_part, c_z, c_all, 0, 0)
    sum_g = Reduction(g_own, g_x, g_part, g_z, g_all, 4, line - owners)

    def spread_h():
        @pl.when(sum_g.owns)
        def _():
            total = sum_g.total()
            g_all[sum_g.rows(x, z), : 2 * size] = total[:, : 2 * size]
            h_pair[0] = total[:, 2 * size :]
            remote(h_pair.at[0], h_pair.at[1], reduce_send.at[8], reduce_recv.at[8], samp=partner)

    def spread_pair():
        @pl.when(sum_g.owns)
        def _():
            arrived(h_pair.at[0], reduce_recv.at[8])
            h_in[y] = h_pair[0] + h_pair[1]
            for step in (2, 1, -1):
                remote(h_in.at[y], h_in.at[y], reduce_send.at[9], reduce_recv.at[9], samp=slot(step))

    def share_g():
        @pl.when(sum_g.owns)
        def _():
            arrived(h_in.at[pl.ds(0, chips - 1)], reduce_recv.at[9])
            g_all[sum_g.rows(x, z), 2 * size :] = jnp.sum(h_in[...], axis=0)
            sum_g.share_z()

    def share_c():
        @pl.when(sum_c.owns)
        def _():
            c_all[sum_c.rows(x, z), :] = sum_c.total()
            sum_c.share_z()

    reference = mine[...]
    g_own[:, 2 * size :] = dot3(split(reference), split(reference * weights(samp)), NT)

    def own_gram(j, carry):
        mass = weights(j)
        for s in range(2):
            value = bases[s, :, columns(j)]
            high, low = split(value)
            at = pl.ds(size * (s + 1), size)
            zh[j, at, :] = high
            zl[j, at, :] = low
            curv[s] += dot3((high, low), split(value * mass), NT)
        return carry


    def cross(j, first=False):
        value = gathered[j]
        high, low = split(value)
        zh[j, pl.ds(0, size), :] = high
        zl[j, pl.ds(0, size), :] = low
        at = pl.ds(size, 2 * size)
        term = dot3(split(value * weights(j)), (zh[j, at, :], zl[j, at, :]), NT)
        if first:
            gram[...] = term
        else:
            gram[...] += term

    curv[...] = jnp.zeros_like(curv)
    load_bases(0).wait()
    lax.fori_loop(0, samps // 2, own_gram, 0)
    from_left, from_right, far = gathered.at[left], gathered.at[right], gathered.at[slot(2)]
    arrived(mine.at[rows(0)], gather_left.at[0])
    sent.append(send(from_left.at[rows(0)], from_left.at[rows(0)], gather_send.at[5], gather_far.at[0], right))
    arrived(mine.at[rows(1)], gather_right.at[1])
    sent.append(send(from_right.at[rows(1)], from_right.at[rows(1)], gather_send.at[6], gather_far.at[1], left))
    load_bases(1).wait()
    lax.fori_loop(samps // 2, samps, own_gram, 0)
    g_own[:, : 2 * size] = pack(curv[0], curv[1])
    sum_g.scatter_x()
    arrived(mine.at[rows(1)], gather_left.at[1])
    sent.append(send(from_left, from_left, gather_send.at[7], gather_pair.at[1], partner))
    arrived(mine.at[rows(0)], gather_right.at[0])
    sent.append(send(from_right, from_right, gather_send.at[8], gather_pair.at[2], partner))
    arrived(mine, gather_pair.at[0])
    cross(samp, True)
    cross(partner)
    cross(left)
    cross(right)
    arrived(mine.at[rows(0)], gather_far.at[0])
    arrived(mine.at[rows(1)], gather_far.at[1])
    sent.append(send(far, far, gather_send.at[9], gather_pair.at[3], partner))
    cross(slot(2))
    for i, step in ((1, -1), (2, 1), (3, 2)):
        arrived(mine, gather_pair.at[i])
        cross(slot(step, True))

    sum_c.scatter_x()
    sum_g.scatter_z()
    sum_c.scatter_z()
    spread_h()
    share_c()
    spread_pair()
    sum_c.share_x()
    share_g()
    sum_c.finish()

    cross_gram = [c_all[:, :size], c_all[:, size:]]
    normal = [exact(c, c, NT) for c in cross_gram]
    minus_inverse = invert(normal, leaf, sum_g.share_x)
    turned = [-exact(m, c) for m, c in zip(minus_inverse, cross_gram)]

    sum_g.finish()
    of_bases = unpack(g_all[:, : 2 * size])
    of_reference = g_all[:, 2 * size :]
    pieces = [split(t) for t in turned]
    middles = [dot3(split(g), p, NT) for g, p in zip(of_bases, pieces)]
    mixed = [dot3(p, split(c), NT) for p, c in zip(pieces, cross_gram)]
    outer = [dot3(p, split(m)) for p, m in zip(pieces, middles)]
    results = series([o - 2.0 * m + of_reference for o, m in zip(outer, mixed)])
    factors = [f * weight_ref[s] for s, f in enumerate(results)]
    plain = -(factors[0] + factors[1])
    finals = [dot3(split(f), p) for f, p in zip(factors, pieces)]
    for s in range(2):
        lhs_h[s + 1], lhs_l[s + 1] = split(finals[s])
    lhs_h[0], lhs_l[0] = split(plain)

    def term(j):
        total = None
        for k in range(3):
            at = pl.ds(size * k, size)
            part = dot3((lhs_h[k], lhs_l[k]), (zh[j, at, :], zl[j, at, :]))
            total = part if total is None else total + part
        return total

    steps = (2, 1, -1, 0)
    for i, step in enumerate(steps):
        pair_out[i] = term(slot(step, True))
        sent.append(send(pair_out.at[i], pair_in.at[i], final_send.at[i], final_pair.at[i], partner))

    def own_term(i):
        value = term(slot(steps[i]))
        arrived(pair_in.at[i], final_pair.at[i])
        return value + pair_in[i]

    def forward(i, h, to, sem, recv, dst):
        sent.append(send(sums.at[i, rows(h)], dst, final_send.at[sem], recv, to))

    sums[0] = own_term(0)
    forward(0, 0, right, 4, final_far.at[0], far_in.at[0])
    forward(0, 1, left, 5, final_far.at[1], far_in.at[1])
    sums[1] = own_term(1)
    forward(1, 1, right, 6, final_near.at[1], near_in.at[0, rows(1)])
    sums[2] = own_term(2)
    forward(2, 0, left, 7, final_near.at[2], near_in.at[1, rows(0)])
    arrived(far_in.at[0], final_far.at[0])
    sums[1, rows(0), :] += far_in[0]
    forward(1, 0, right, 8, final_near.at[0], near_in.at[0, rows(0)])
    arrived(far_in.at[1], final_far.at[1])
    sums[2, rows(1), :] += far_in[1]
    forward(2, 1, left, 9, final_near.at[3], near_in.at[1, rows(1)])
    out_ref[...] = own_term(3)
    for i in range(4):
        arrived(far_in.at[0], final_near.at[i])
    out_ref[...] += near_in[0] + near_in[1]

    for copy in sent:
        copy.wait_send()
    sum_c.drain()
    sum_g.drain()

    @pl.when(sum_g.owns)
    def _():
        arrived(h_pair.at[0], reduce_send.at[8])
        arrived(h_in.at[pl.ds(0, chips - 1)], reduce_send.at[9])


def body(bases, reference_basis, mass, interp_weights):
    cells, samps = lax.axis_size("cell"), lax.axis_size("samp")
    count, depth, size = bases.shape
    block = reference_basis.shape[0]
    packed, wide = 2 * size, 3 * size
    half = size // 2
    hbm, vmem = pl.BlockSpec(memory_space=pltpu.HBM), pl.BlockSpec(memory_space=pltpu.VMEM)
    line = 8
    lines = cells // line
    result = pl.pallas_call(
        functools.partial(kernel, cells, depth * cells, samps),
        out_shape=jax.ShapeDtypeStruct((size, block), F32),
        in_specs=[hbm] * 4,
        out_specs=vmem,
        scratch_shapes=[
            pltpu.VMEM((count, size, depth), F32),
            pltpu.VMEM((1, depth), F32),
            pltpu.SMEM((count,), F32),
            pltpu.VMEM((samps, size, block), F32),
            pltpu.VMEM((samps, 3 * size, block), BF16),
            pltpu.VMEM((samps, 3 * size, block), BF16),
            pltpu.VMEM((size, packed), F32),
            pltpu.VMEM((2, size, size), F32),
            pltpu.VMEM((lines, size // lines, packed), F32),
            pltpu.VMEM((size // lines, packed), F32),
            pltpu.VMEM((line, 8, packed), F32),
            pltpu.VMEM((size, packed), F32),
            pltpu.VMEM((size, wide), F32),
            pltpu.VMEM((lines, size // lines, wide), F32),
            pltpu.VMEM((size // lines, wide), F32),
            pltpu.VMEM((line, 8, wide), F32),
            pltpu.VMEM((2, 8, size), F32),
            pltpu.VMEM((samps // 2, 8, size), F32),
            pltpu.VMEM((size, wide), F32),
            pltpu.VMEM((LEAF, 2 * LEAF), F32),
            pltpu.VMEM((3, size, size), BF16),
            pltpu.VMEM((3, size, size), BF16),
            pltpu.VMEM((4, size, block), F32),
            pltpu.VMEM((4, size, block), F32),
            pltpu.VMEM((3, size, block), F32),
            pltpu.VMEM((2, half, block), F32),
            pltpu.VMEM((2, size, block), F32),
            pltpu.SemaphoreType.DMA((5,)),
            pltpu.SemaphoreType.DMA((10,)),
            pltpu.SemaphoreType.DMA((2,)),
            pltpu.SemaphoreType.DMA((2,)),
            pltpu.SemaphoreType.DMA((2,)),
            pltpu.SemaphoreType.DMA((4,)),
            pltpu.SemaphoreType.DMA((10,)),
            pltpu.SemaphoreType.DMA((10,)),
            pltpu.SemaphoreType.DMA((10,)),
            pltpu.SemaphoreType.DMA((4,)),
            pltpu.SemaphoreType.DMA((2,)),
            pltpu.SemaphoreType.DMA((4,)),
        ],
        compiler_params=pltpu.CompilerParams(
            collective_id=0, has_side_effects=True, vmem_limit_bytes=48 * 1024 * 1024
        ),
    )(jnp.swapaxes(bases, 1, 2), reference_basis.T, mass[None, :], interp_weights)
    return result.T


def solution(mesh):
    placed = (P("samp", "cell", None), P(("cell", "samp"), None), P("cell"), P("samp"))
    return jax.shard_map(
        body, mesh=mesh, in_specs=placed, out_specs=P(("cell", "samp"), None), check_vma=False
    )
```

```python
import functools

import jax
import jax.numpy as jnp
from jax import lax
from jax.experimental import pallas as pl
from jax.experimental.pallas import tpu as pltpu
from jax.sharding import PartitionSpec as P

NTERMS = 6
MESH = pl.DeviceIdType.MESH
F32, BF16 = jnp.float32, jnp.bfloat16
HIGHEST = lax.Precision.HIGHEST
NN = (((1,), (0,)), ((), ()))
NT = (((1,), (1,)), ((), ()))
LEAF = 64


def split(x):
    high = x.astype(BF16)
    return high, (x - high.astype(F32)).astype(BF16)


def dot(a, b, dims=NN):
    return lax.dot_general(a, b, dims, preferred_element_type=F32)


def dot3(a, b, dims=NN):
    (ah, al), (bh, bl) = a, b
    return dot(ah, bh, dims) + (dot(ah, bl, dims) + dot(al, bh, dims))


def matmul(a, b):
    return dot3(split(a), split(b))


def exact(a, b, dims=NN):
    return lax.dot_general(a, b, dims, precision=HIGHEST, preferred_element_type=F32)


def pack(first, second):
    middle = jnp.concatenate([first[:, 128:], second[:, 128:]], axis=1)
    return jnp.concatenate([first[:, :128], middle, second[:, :128]], axis=1)


def unpack(packed):
    middle = packed[:, 128:256]
    half = middle.shape[1] // 2
    first = jnp.concatenate([packed[:, :128], middle[:, :half]], axis=1)
    second = jnp.concatenate([packed[:, 256:384], middle[:, half:]], axis=1)
    return first, second


def sweep_leaf(leaf_ref):
    lane = lax.broadcasted_iota(jnp.int32, (8, 128), 1)
    row = lax.broadcasted_iota(jnp.int32, (8, 128), 0)
    within = lane & (LEAF - 1)
    start = lane - within

    def step(p, carry):
        first = 8 * p
        index = [start + first + c for c in range(8)]
        own = pl.ds(pl.multiple_of(first, 8), 8)
        pivot = leaf_ref[own, :]

        def column(x, c):
            return jnp.take_along_axis(x, index[c], axis=1, mode="promise_in_bounds")

        columns = [column(pivot, c) for c in range(8)]
        e = {
            (r, c): jnp.broadcast_to(columns[c][r : r + 1, :], (8, 128))
            for c in range(8)
            for r in range(c + 1)
        }

        def at(r, c):
            return (r, c) if r <= c else (c, r)

        for k in range(8):
            inverse = 1.0 / e[k, k]
            scaled = {j: e[at(k, j)] * inverse for j in range(8) if j != k}
            for j in range(8):
                for i in range(j + 1):
                    if i != k and j != k:
                        e[i, j] = e[i, j] - e[at(i, k)] * scaled[j]
            for j in scaled:
                e[at(k, j)] = scaled[j]
            e[k, k] = -inverse

        inside = (within >= first) & (within < first + 8)
        rows = [
            jnp.where(
                within == first + c,
                1.0,
                jnp.where(inside, 0.0, -jnp.broadcast_to(pivot[c : c + 1, :], (8, 128))),
            )
            for c in range(8)
        ]
        scaled_rows = []
        for r in range(8):
            total = e[at(r, 0)] * rows[0]
            for c in range(1, 8):
                total = total + e[at(r, c)] * rows[c]
            scaled_rows.append(total)
        for g in range(LEAF // 8):
            block = leaf_ref[8 * g : 8 * g + 8, :]
            total = jnp.where(inside, 0.0, block)
            for c in range(8):
                total = total - column(block, c) * scaled_rows[c]
            leaf_ref[8 * g : 8 * g + 8, :] = total
        joined = scaled_rows[0]
        for r in range(1, 8):
            joined = jnp.where(row == r, scaled_rows[r], joined)
        leaf_ref[own, :] = joined
        return carry

    lax.fori_loop(0, LEAF // 8, step, 0)


def solve(normal, right, leaf_ref, between):
    size = normal[0].shape[0]
    pivots = [n[:, :LEAF] for n in normal]
    rests = [jnp.concatenate([r, n[:, LEAF:]], axis=1) for n, r in zip(normal, right)]
    for i in range(size // LEAF):
        own = slice(LEAF * i, LEAF * (i + 1))
        leaf_ref[...] = jnp.concatenate([p[own] for p in pivots], axis=1)
        sweep_leaf(leaf_ref)
        if i == 0:
            between()
        minus_inverse = leaf_ref[...]
        minus_rows = [exact(minus_inverse[:, LEAF * s : LEAF * (s + 1)], rests[s][own]) for s in range(2)]
        products = [exact(p, r) for p, r in zip(pivots, minus_rows)]
        updated = []
        for rest, rows, product in zip(rests, minus_rows, products):
            new = rest + product
            parts = [new[: LEAF * i], -rows, new[LEAF * (i + 1) :]]
            updated.append(jnp.concatenate([part for part in parts if part.shape[0]], axis=0))
        pivots = [u[:, size : size + LEAF] for u in updated]
        rests = [
            jnp.concatenate([u[:, :size], u[:, size + LEAF :]], axis=1) if u.shape[1] > size + LEAF else u[:, :size]
            for u in updated
        ]
    return rests


def series(curvatures):
    size = curvatures[0].shape[0]
    diagonal = lax.broadcasted_iota(jnp.int32, (size, size), 0) == lax.broadcasted_iota(jnp.int32, (size, size), 1)
    weight = [(-1.0) ** n / (2 * n + 1) for n in range(NTERMS)]

    def pair(curvature, n):
        return weight[n + 1] * curvature + jnp.where(diagonal, weight[n], 0.0)

    pieces = [split(c) for c in curvatures]
    squares = [split(dot3(p, p)) for p in pieces]
    results = [pair(c, NTERMS - 2) for c in curvatures]
    for n in range(NTERMS - 4, -1, -2):
        products = [dot3(square, split(r)) for square, r in zip(squares, results)]
        results = [pair(c, n) + product for c, product in zip(curvatures, products)]
    return results


def kernel(
    cells,
    depth,
    samps,
    bases_hbm,
    own_hbm,
    mass_hbm,
    weight_hbm,
    out_ref,
    bases,
    mass_row,
    weight_ref,
    gathered,
    zh,
    zl,
    gram,
    curv,
    c_x,
    c_part,
    c_z,
    c_all,
    g_own,
    g_x,
    g_part,
    g_z,
    h_pair,
    h_in,
    g_all,
    leaf,
    lhs_h,
    lhs_l,
    pair_out,
    pair_in,
    sums,
    far_in,
    near_in,
    load_sem,
    gather_send,
    gather_left,
    gather_right,
    gather_far,
    gather_pair,
    reduce_send,
    reduce_recv,
    final_send,
    final_pair,
    final_far,
    final_near,
):
    size, block = own_hbm.shape
    half = size // 2
    cell = lax.axis_index("cell")
    samp = lax.axis_index("samp")
    chips = samps // 2
    core = lax.rem(samp, 2)
    y = samp // 2
    line = 8
    lines = cells // line
    x, z = cell // line, lax.rem(cell, line)

    def there(step):
        return lax.rem(y + step + chips, chips)

    def slot(step, other=False):
        return 2 * there(step) + (1 - core if other else core)

    partner, right, left = slot(0, True), slot(1), slot(-1)

    def columns(j):
        return pl.ds(pl.multiple_of(j * block, block), block)

    def load_bases(h):
        at = pl.ds(h * block * (samps // 2), block * (samps // 2))
        return pltpu.make_async_copy(bases_hbm.at[:, :, at], bases.at[:, :, at], load_sem.at[h])

    loads = [
        pltpu.make_async_copy(mass_hbm, mass_row, load_sem.at[2]),
        pltpu.make_async_copy(own_hbm, gathered.at[samp], load_sem.at[3]),
        pltpu.make_async_copy(weight_hbm, weight_ref, load_sem.at[4]),
    ]
    for load in loads:
        load.start()

    barrier = pltpu.get_barrier_semaphore()

    def along_x(d):
        return lax.rem(x + d, lines) * line + z

    def along_z(d):
        return x * line + lax.rem(z + d, line)

    for friend in (right, left, partner, slot(2)):
        pl.semaphore_signal(barrier, inc=1, device_id={"samp": friend}, device_id_type=MESH)
    for d in range(1, line):
        pl.semaphore_signal(barrier, inc=1, device_id={"cell": along_z(d)}, device_id_type=MESH)
    for d in range(1, lines):
        pl.semaphore_signal(barrier, inc=1, device_id={"cell": along_x(d)}, device_id_type=MESH)

    def weights(j):
        return mass_row[:, columns(j)] * (1.0 / depth)

    for load in loads:
        load.wait()
    mine = gathered.at[samp]
    pl.semaphore_wait(barrier, lines + line + chips - 2)

    def remote(src, dst, send_sem, recv_sem, **to):
        copy = pltpu.make_async_remote_copy(
            src_ref=src, dst_ref=dst, send_sem=send_sem, recv_sem=recv_sem, device_id=to, device_id_type=MESH
        )
        copy.start()
        return copy

    def send(src, dst, send_sem, recv_sem, to):
        return remote(src, dst, send_sem, recv_sem, samp=to)

    def arrived(ref, sem):
        pltpu.make_async_copy(ref, ref, sem).wait()

    def rows(h):
        return pl.ds(half * h, half)

    sent = []
    for h in (0, 1):
        sent.append(send(mine.at[rows(h)], mine.at[rows(h)], gather_send.at[h], gather_left.at[h], right))
        sent.append(send(mine.at[rows(1 - h)], mine.at[rows(1 - h)], gather_send.at[3 - h], gather_right.at[1 - h], left))
    sent.append(send(mine, mine, gather_send.at[4], gather_pair.at[0], partner))

    for h in (0, 1):
        load_bases(h).start()

    quarter = size // lines
    owners = quarter // 8

    class Reduction:
        def __init__(self, own, x_in, part, z_in, whole, sem, shift):
            self.own, self.x_in, self.part, self.z_in, self.whole = own, x_in, part, z_in, whole
            self.sent = [reduce_send.at[sem + i] for i in range(4)]
            self.recv = [reduce_recv.at[sem + i] for i in range(4)]
            self.shift = shift
            self.owns = self.is_owner(z)

        def is_owner(self, z_of):
            return (z_of >= self.shift) & (z_of < self.shift + owners)

        def rows(self, x_of, z_of=None):
            if z_of is None:
                return pl.ds(pl.multiple_of(quarter * x_of, 8), quarter)
            return pl.ds(pl.multiple_of(quarter * x_of + 8 * (z_of - self.shift), 8), 8)

        def small(self, z_of):
            return pl.ds(pl.multiple_of(8 * (z_of - self.shift), 8), 8)

        def count(self, n):
            return self.own.at[pl.ds(0, n)]

        def counted(self, owner, rest, sem):
            @pl.when(self.owns)
            def _():
                arrived(self.count(owner), sem)

            if rest:

                @pl.when(jnp.logical_not(self.owns))
                def _():
                    arrived(self.count(rest), sem)

        def scatter_x(self):
            for d in (2, 1, 3):
                to = lax.rem(x + d, lines)
                remote(self.own.at[self.rows(to)], self.x_in.at[x], self.sent[0], self.recv[0], cell=to * line + z)

        def scatter_z(self):
            self.x_in[x] = self.own[self.rows(x), :]
            arrived(self.count(quarter * (lines - 1)), self.recv[0])
            self.part[...] = jnp.sum(self.x_in[...], axis=0)
            for d in (4, 3, 5, 2, 6, 1, 7):
                to = lax.rem(z + d, line)

                @pl.when(self.is_owner(to))
                def _(to=to):
                    src = self.part.at[self.small(to)]
                    remote(src, self.z_in.at[z], self.sent[1], self.recv[1], cell=x * line + to)

        def total(self):
            self.z_in[z] = self.part[self.small(z), :]
            arrived(self.count(8 * (line - 1)), self.recv[1])
            return jnp.sum(self.z_in[...], axis=0)

        def share_z(self):
            piece = self.whole.at[self.rows(x, z)]
            for d in (4, 3, 5, 2, 6, 1, 7):
                remote(piece, piece, self.sent[2], self.recv[2], cell=along_z(d))

        def share_x(self):
            self.counted(quarter - 8, quarter, self.recv[2])
            piece = self.whole.at[self.rows(x)]
            for d in (2, 1, 3):
                remote(piece, piece, self.sent[3], self.recv[3], cell=along_x(d))

        def finish(self):
            arrived(self.count(quarter * (lines - 1)), self.recv[3])

        def drain(self):
            arrived(self.count(quarter * (lines - 1)), self.sent[0])
            self.counted(quarter - 8, quarter, self.sent[1])
            self.counted(8 * (line - 1), 0, self.sent[2])
            arrived(self.count(quarter * (lines - 1)), self.sent[3])

    sum_c = Reduction(gram, c_x, c_part, c_z, c_all, 0, 0)
    sum_g = Reduction(g_own, g_x, g_part, g_z, g_all, 4, line - owners)

    def spread_h():
        @pl.when(sum_g.owns)
        def _():
            total = sum_g.total()
            g_all[sum_g.rows(x, z), : 2 * size] = total[:, : 2 * size]
            h_pair[0] = total[:, 2 * size :]
            remote(h_pair.at[0], h_pair.at[1], reduce_send.at[8], reduce_recv.at[8], samp=partner)

    def spread_pair():
        @pl.when(sum_g.owns)
        def _():
            arrived(h_pair.at[0], reduce_recv.at[8])
            h_in[y] = h_pair[0] + h_pair[1]
            for step in (2, 1, -1):
                remote(h_in.at[y], h_in.at[y], reduce_send.at[9], reduce_recv.at[9], samp=slot(step))

    def share_g():
        @pl.when(sum_g.owns)
        def _():
            arrived(h_in.at[pl.ds(0, chips - 1)], reduce_recv.at[9])
            g_all[sum_g.rows(x, z), 2 * size :] = jnp.sum(h_in[...], axis=0)
            sum_g.share_z()

    def share_c():
        @pl.when(sum_c.owns)
        def _():
            c_all[sum_c.rows(x, z), :] = sum_c.total()
            sum_c.share_z()

    reference = mine[...]
    g_own[:, 2 * size :] = dot3(split(reference), split(reference * weights(samp)), NT)

    def own_gram(j, carry):
        mass = weights(j)
        for s in range(2):
            value = bases[s, :, columns(j)]
            high, low = split(value)
            at = pl.ds(size * (s + 1), size)
            zh[j, at, :] = high
            zl[j, at, :] = low
            curv[s] += dot3((high, low), split(value * mass), NT)
        return carry


    def cross(j, first=False):
        value = gathered[j]
        high, low = split(value)
        zh[j, pl.ds(0, size), :] = high
        zl[j, pl.ds(0, size), :] = low
        at = pl.ds(size, 2 * size)
        term = dot3(split(value * weights(j)), (zh[j, at, :], zl[j, at, :]), NT)
        if first:
            gram[...] = term
        else:
            gram[...] += term

    curv[...] = jnp.zeros_like(curv)
    load_bases(0).wait()
    lax.fori_loop(0, samps // 2, own_gram, 0)
    from_left, from_right, far = gathered.at[left], gathered.at[right], gathered.at[slot(2)]
    arrived(mine.at[rows(0)], gather_left.at[0])
    sent.append(send(from_left.at[rows(0)], from_left.at[rows(0)], gather_send.at[5], gather_far.at[0], right))
    arrived(mine.at[rows(1)], gather_right.at[1])
    sent.append(send(from_right.at[rows(1)], from_right.at[rows(1)], gather_send.at[6], gather_far.at[1], left))
    load_bases(1).wait()
    lax.fori_loop(samps // 2, samps, own_gram, 0)
    g_own[:, : 2 * size] = pack(curv[0], curv[1])
    sum_g.scatter_x()
    arrived(mine.at[rows(1)], gather_left.at[1])
    sent.append(send(from_left, from_left, gather_send.at[7], gather_pair.at[1], partner))
    arrived(mine.at[rows(0)], gather_right.at[0])
    sent.append(send(from_right, from_right, gather_send.at[8], gather_pair.at[2], partner))
    arrived(mine, gather_pair.at[0])
    cross(samp, True)
    cross(partner)
    cross(left)
    cross(right)
    arrived(mine.at[rows(0)], gather_far.at[0])
    arrived(mine.at[rows(1)], gather_far.at[1])
    sent.append(send(far, far, gather_send.at[9], gather_pair.at[3], partner))
    cross(slot(2))
    for i, step in ((1, -1), (2, 1), (3, 2)):
        arrived(mine, gather_pair.at[i])
        cross(slot(step, True))

    sum_c.scatter_x()
    sum_g.scatter_z()
    sum_c.scatter_z()
    spread_h()
    share_c()
    spread_pair()
    sum_c.share_x()
    share_g()
    sum_c.finish()

    cross_gram = [c_all[:, :size], c_all[:, size:]]
    normal = [exact(c, c, NT) for c in cross_gram]
    turned = solve(normal, cross_gram, leaf, sum_g.share_x)

    sum_g.finish()
    of_bases = unpack(g_all[:, : 2 * size])
    of_reference = g_all[:, 2 * size :]
    pieces = [split(t) for t in turned]
    middles = [dot3(split(g), p, NT) for g, p in zip(of_bases, pieces)]
    mixed = [dot3(p, split(c), NT) for p, c in zip(pieces, cross_gram)]
    outer = [dot3(p, split(m)) for p, m in zip(pieces, middles)]
    results = series([o - 2.0 * m + of_reference for o, m in zip(outer, mixed)])
    factors = [f * weight_ref[s] for s, f in enumerate(results)]
    plain = -(factors[0] + factors[1])
    finals = [dot3(split(f), p) for f, p in zip(factors, pieces)]
    for s in range(2):
        lhs_h[s + 1], lhs_l[s + 1] = split(finals[s])
    lhs_h[0], lhs_l[0] = split(plain)

    def term(j):
        total = None
        for k in range(3):
            at = pl.ds(size * k, size)
            part = dot3((lhs_h[k], lhs_l[k]), (zh[j, at, :], zl[j, at, :]))
            total = part if total is None else total + part
        return total

    steps = (2, 1, -1, 0)
    for i, step in enumerate(steps):
        pair_out[i] = term(slot(step, True))
        sent.append(send(pair_out.at[i], pair_in.at[i], final_send.at[i], final_pair.at[i], partner))

    def own_term(i):
        value = term(slot(steps[i]))
        arrived(pair_in.at[i], final_pair.at[i])
        return value + pair_in[i]

    def forward(i, h, to, sem, recv, dst):
        sent.append(send(sums.at[i, rows(h)], dst, final_send.at[sem], recv, to))

    sums[0] = own_term(0)
    forward(0, 0, right, 4, final_far.at[0], far_in.at[0])
    forward(0, 1, left, 5, final_far.at[1], far_in.at[1])
    sums[1] = own_term(1)
    forward(1, 1, right, 6, final_near.at[1], near_in.at[0, rows(1)])
    sums[2] = own_term(2)
    forward(2, 0, left, 7, final_near.at[2], near_in.at[1, rows(0)])
    arrived(far_in.at[0], final_far.at[0])
    sums[1, rows(0), :] += far_in[0]
    forward(1, 0, right, 8, final_near.at[0], near_in.at[0, rows(0)])
    arrived(far_in.at[1], final_far.at[1])
    sums[2, rows(1), :] += far_in[1]
    forward(2, 1, left, 9, final_near.at[3], near_in.at[1, rows(1)])
    out_ref[...] = own_term(3)
    for i in range(4):
        arrived(far_in.at[0], final_near.at[i])
    out_ref[...] += near_in[0] + near_in[1]

    for copy in sent:
        copy.wait_send()
    sum_c.drain()
    sum_g.drain()

    @pl.when(sum_g.owns)
    def _():
        arrived(h_pair.at[0], reduce_send.at[8])
        arrived(h_in.at[pl.ds(0, chips - 1)], reduce_send.at[9])


def body(bases, reference_basis, mass, interp_weights):
    cells, samps = lax.axis_size("cell"), lax.axis_size("samp")
    count, depth, size = bases.shape
    block = reference_basis.shape[0]
    packed, wide = 2 * size, 3 * size
    half = size // 2
    hbm, vmem = pl.BlockSpec(memory_space=pltpu.HBM), pl.BlockSpec(memory_space=pltpu.VMEM)
    line = 8
    lines = cells // line
    result = pl.pallas_call(
        functools.partial(kernel, cells, depth * cells, samps),
        out_shape=jax.ShapeDtypeStruct((size, block), F32),
        in_specs=[hbm] * 4,
        out_specs=vmem,
        scratch_shapes=[
            pltpu.VMEM((count, size, depth), F32),
            pltpu.VMEM((1, depth), F32),
            pltpu.SMEM((count,), F32),
            pltpu.VMEM((samps, size, block), F32),
            pltpu.VMEM((samps, 3 * size, block), BF16),
            pltpu.VMEM((samps, 3 * size, block), BF16),
            pltpu.VMEM((size, packed), F32),
            pltpu.VMEM((2, size, size), F32),
            pltpu.VMEM((lines, size // lines, packed), F32),
            pltpu.VMEM((size // lines, packed), F32),
            pltpu.VMEM((line, 8, packed), F32),
            pltpu.VMEM((size, packed), F32),
            pltpu.VMEM((size, wide), F32),
            pltpu.VMEM((lines, size // lines, wide), F32),
            pltpu.VMEM((size // lines, wide), F32),
            pltpu.VMEM((line, 8, wide), F32),
            pltpu.VMEM((2, 8, size), F32),
            pltpu.VMEM((samps // 2, 8, size), F32),
            pltpu.VMEM((size, wide), F32),
            pltpu.VMEM((LEAF, 2 * LEAF), F32),
            pltpu.VMEM((3, size, size), BF16),
            pltpu.VMEM((3, size, size), BF16),
            pltpu.VMEM((4, size, block), F32),
            pltpu.VMEM((4, size, block), F32),
            pltpu.VMEM((3, size, block), F32),
            pltpu.VMEM((2, half, block), F32),
            pltpu.VMEM((2, size, block), F32),
            pltpu.SemaphoreType.DMA((5,)),
            pltpu.SemaphoreType.DMA((10,)),
            pltpu.SemaphoreType.DMA((2,)),
            pltpu.SemaphoreType.DMA((2,)),
            pltpu.SemaphoreType.DMA((2,)),
            pltpu.SemaphoreType.DMA((4,)),
            pltpu.SemaphoreType.DMA((10,)),
            pltpu.SemaphoreType.DMA((10,)),
            pltpu.SemaphoreType.DMA((10,)),
            pltpu.SemaphoreType.DMA((4,)),
            pltpu.SemaphoreType.DMA((2,)),
            pltpu.SemaphoreType.DMA((4,)),
        ],
        compiler_params=pltpu.CompilerParams(
            collective_id=0, has_side_effects=True, vmem_limit_bytes=48 * 1024 * 1024
        ),
    )(jnp.swapaxes(bases, 1, 2), reference_basis.T, mass[None, :], interp_weights)
    return result.T


def solution(mesh):
    placed = (P("samp", "cell", None), P(("cell", "samp"), None), P("cell"), P("samp"))
    return jax.shard_map(
        body, mesh=mesh, in_specs=placed, out_specs=P(("cell", "samp"), None), check_vma=False
    )
```
